256 devices in a mesh: seq: 64 (over y_hi, z, x), chan: 4 (over y_lo, core).
Axes of the slice: x: 4, y: 4 (y_hi: 2, y_lo: 2; y = y_hi * 2 + y_lo), z: 8, core: 2. Of those that a mesh axis runs over, the one named last changes fastest.
Arguments:
- pre_gate: bfloat16 [16384, 4096], P('seq', 'chan'), may hold values from -6 to 6
- post_gate: bfloat16 [16384, 4096], P('seq', 'chan'), may hold values from -6 to 6
- values: bfloat16 [16384, 4096], P('seq', 'chan'), may hold values from -6 to 6
- decay_rates: float32 [4096, 16], P('chan'), may hold values from 1.2207031e-06 to 0.03
- residues: float32 [4096, 16], P('chan'), may hold values from -1.5 to 1.5
- skip_gain: float32 [4096], P('chan'), may hold values from -1 to 1
- out_weight: bfloat16 [4096, 4096], P('chan'), may hold values from -0.125 to 0.125
Outputs:
- mixed: bfloat16 [16384, 4096], P('seq', 'chan')
The draws below stay inside these ranges and needn't reach their ends.
All inputs are finite; a program needn't handle non-finite values.
Results may differ from the reference program's by a relative error of at most 0.02.
Values may be sent and summed in bfloat16 or wider, within the bound.
No kernel may reach another device: no remote copies, remote signals or barrier semaphores. Data moves between devices by JAX's collectives and lax.ppermute only.
A program may use at most 128 MiB of HBM per device.

```python
import math
import jax
import jax.numpy as jnp
from jax import lax

C = 4096
DOUT = 4096
MODES = 16
TOKENS = 16384


def with_spikes(array, stream_key, source, target, shards_of, factor):
    owner, partner = [(jnp.arange(array.shape[dim]) // (array.shape[dim] // shards_of)).reshape([-1 if axis == dim else 1 for axis in range(array.ndim)]) for dim in (source, target)]
    chosen = jax.random.permutation(stream_key, shards_of)[partner]
    strong = (owner == chosen) | (owner == (partner + shards_of // 2) % shards_of)
    return jnp.where(strong, factor * array, array)


def block_levels(rng, extent, cuts, smallest, high):
    def one(position, blocks):
        heights = jax.random.uniform(jax.random.fold_in(jax.random.fold_in(rng, 6), position), (blocks,), jnp.float32, smallest / len(cuts), high / len(cuts))
        return jnp.repeat(jnp.exp(heights), extent[position] // blocks).reshape((-1,) + (1,) * (len(extent) - position - 1))

    gain = one(*cuts[0])
    for cut in cuts[1:]:
        gain = gain * one(*cut)
    return gain


def bell_draw(rng, shape, scale, limit, shards=(), held_as=jnp.bfloat16):
    array = jax.random.normal(rng, shape, jnp.float32) * scale
    if len(shards) > 0:
        array = block_levels(rng, shape, shards, -0.22, 0.18) * array
    return jnp.clip(array, min=-limit, max=limit).astype(held_as)


def heavy_noise(own_key, shape, spread, reach, cuts, heavy, kind=jnp.bfloat16):
    drawn = spread * jax.random.normal(own_key, shape, jnp.float32)
    if cuts:
        drawn = drawn * block_levels(own_key, shape, cuts, -0.22, 0.18)
    return jnp.clip(with_spikes(drawn, jax.random.fold_in(own_key, 3), *heavy), -reach, reach).astype(kind)


def setup_inputs(seed: int = 0) -> dict:
    key_list = jax.random.split(jax.random.key(seed), 8)
    pre_gate = bell_draw(key_list[0], (TOKENS, C), 1.0, 6.0, ((0, 64), (1, 4)))
    post_gate = bell_draw(key_list[1], (TOKENS, C), 1.0, 6.0, ((0, 64), (1, 4)))
    values = bell_draw(key_list[2], (TOKENS, C), 1.0, 6.0, ((0, 64), (1, 4)))
    decay_rates = jnp.clip(jnp.exp(math.log(0.03) - 10.109526 * jax.random.uniform(key_list[3], (C, MODES), jnp.float32) ** block_levels(key_list[3], (C, MODES), ((0, 4),), -0.2, 0.2)), 1.220703097715159e-06, 0.03)
    residues = bell_draw(key_list[4], (C, MODES), MODES ** -0.5, 1.5, ((0, 4),), jnp.float32)
    skip_gain = jnp.clip(jax.random.uniform(key_list[5], (C,), jnp.float32, -1.0, 1.0) * block_levels(key_list[5], (C,), ((0, 4),), -0.4, 0.0), -1.0, 1.0)
    out_weight = heavy_noise(key_list[6], (C, DOUT), C ** -0.5, 0.125, ((0, 4),), (0, 1, 4, 2.0))
    return dict(pre_gate=pre_gate, post_gate=post_gate, values=values, decay_rates=decay_rates, residues=residues, skip_gain=skip_gain, out_weight=out_weight)


def block_conv(pieces):
    signal, decay_block, residue_block = pieces
    seq_total = signal.shape[0]
    positions = jnp.arange(seq_total).astype(jnp.float32)

    def add_mode(mode_index, running):
        decay_rate = decay_block[:, mode_index]
        weight_c = residue_block[:, mode_index] * jnp.sqrt(-jnp.expm1(-2.0 * decay_rate))
        return running + weight_c[None, :] * jnp.exp(-decay_rate[None, :] * positions[:, None])
    impulse = lax.fori_loop(0, decay_block.shape[1], add_mode, jnp.zeros(signal.shape, jnp.float32))
    spectrum = jnp.fft.rfft(signal.astype(jnp.float32), n=2 * seq_total, axis=0) * jnp.fft.rfft(impulse, n=2 * seq_total, axis=0)
    return jnp.fft.irfft(spectrum, n=2 * seq_total, axis=0)[:seq_total]

def reference(pre_gate, post_gate, values, decay_rates, residues, skip_gain, out_weight):
    seq_total, channels = pre_gate.shape
    inner = (pre_gate.astype(jnp.float32) * values.astype(jnp.float32)).astype(jnp.bfloat16)
    width_block = min(256, channels)
    groups = channels // width_block
    signal = inner.reshape(seq_total, groups, width_block).transpose(1, 0, 2)
    conv = lax.map(block_conv, (signal, decay_rates.reshape(groups, width_block, -1), residues.reshape(groups, width_block, -1)))
    conv = conv.transpose(1, 0, 2).reshape(seq_total, channels)
    mixed_in = conv + skip_gain[None, :] * inner.astype(jnp.float32)
    gated = (post_gate.astype(jnp.float32) * mixed_in).astype(jnp.bfloat16)
    return jnp.dot(gated, out_weight, preferred_element_type=jnp.float32).astype(jnp.bfloat16)
```

```python
import functools

import jax
import jax.numpy as jnp
from jax import lax
from jax.experimental import pallas as pl
from jax.experimental.pallas import tpu as pltpu
from jax.sharding import Mesh
from jax.sharding import PartitionSpec as P

Y_HI, Z, X, Y_LO, CORE = 2, 8, 4, 2, 2
MODES = 16
ROWS = 256
SUBS = 8
STEPS = ROWS // SUBS
LANES = 128


def rows8(row):
    return jnp.broadcast_to(row, (SUBS, row.shape[-1]))


def inner_of(pre_ref, val_ref):
    product = pre_ref[...].astype(jnp.float32) * val_ref[...].astype(jnp.float32)
    return product.astype(jnp.bfloat16).astype(jnp.float32)


def states_kernel(pre_ref, val_ref, rate_ref, sub_ref, total_ref, inner_buf):
    inner_buf[...] = inner_of(pre_ref, val_ref)
    decay = jnp.exp(-rate_ref[...])
    factors = [rows8(decay[m : m + 1]) for m in range(MODES)]
    states = None
    for step in range(STEPS):
        value = inner_buf[pl.ds(step, SUBS, stride=STEPS), :]
        if states is None:
            states = [value] * MODES
        else:
            states = [f * s + value for f, s in zip(factors, states)]
    left = (SUBS - 1 - lax.broadcasted_iota(jnp.int32, (SUBS, LANES), 0)) * STEPS
    left = left.astype(jnp.float32)
    for m in range(MODES):
        sub_ref[m] = states[m]
        weight = jnp.exp(-rows8(rate_ref[m : m + 1]) * left)
        total_ref[m : m + 1, :] = jnp.sum(states[m] * weight, axis=0, keepdims=True)


def local_kernel(pre_ref, val_ref, rate_ref, weight_ref, skip_ref, sub_ref, out_ref, inner_buf, taps_buf):
    inner_buf[...] = inner_of(pre_ref, val_ref)
    lag = lax.broadcasted_iota(jnp.int32, (STEPS, LANES), 0).astype(jnp.float32)
    taps = jnp.zeros((STEPS, LANES), jnp.float32)
    for m in range(MODES):
        taps = taps + weight_ref[m : m + 1] * jnp.exp(-rate_ref[m : m + 1] * lag)
    first = lax.broadcasted_iota(jnp.int32, (STEPS, LANES), 0) == 0
    taps_buf[...] = taps + jnp.where(first, skip_ref[...], 0.0)
    where = lax.broadcasted_iota(jnp.int32, (SUBS, LANES), 0)
    entering = []
    factors = []
    for m in range(MODES):
        rate = rows8(rate_ref[m : m + 1])
        state = sub_ref[m]
        span = 1
        while span < SUBS:
            moved = jnp.where(where >= span, pltpu.roll(state, span, 0), 0.0)
            state = state + jnp.exp(-rate * float(span * STEPS)) * moved
            span *= 2
        state = jnp.where(where >= 1, pltpu.roll(state, 1, 0), 0.0)
        factor = jnp.exp(-rate)
        factors.append(factor)
        entering.append(state * factor * rows8(weight_ref[m : m + 1]))
    for step in range(STEPS):
        total = functools.reduce(lambda a, b: a + b, entering)
        for back in range(step + 1):
            total = total + rows8(taps_buf[back : back + 1]) * inner_buf[pl.ds(step - back, SUBS, stride=STEPS), :]
        out_ref[pl.ds(step, SUBS, stride=STEPS), :] = total
        entering = [f * e for f, e in zip(factors, entering)]


def carry_kernel(local_ref, post_ref, rate_ref, weight_ref, carry_ref, out_ref):
    ahead = (lax.broadcasted_iota(jnp.int32, (SUBS, LANES), 0) + 1).astype(jnp.float32)
    terms = []
    factors = []
    for m in range(MODES):
        rate = rows8(rate_ref[m : m + 1])
        terms.append(jnp.exp(-rate * ahead) * rows8(weight_ref[m : m + 1] * carry_ref[m : m + 1]))
        factors.append(jnp.exp(-rate * float(SUBS)))
    for pair in range(ROWS // (2 * SUBS)):
        sums = []
        for _ in range(2):
            sums.append(functools.reduce(lambda a, b: a + b, terms))
            terms = [f * t for f, t in zip(factors, terms)]
        rows = pl.ds(pair * 2 * SUBS, 2 * SUBS)
        conv = local_ref[rows, :] + jnp.concatenate(sums, axis=0)
        out_ref[rows, :] = (post_ref[rows, :].astype(jnp.float32) * conv).astype(jnp.bfloat16)


def column(rows):
    return pl.BlockSpec((rows, LANES), lambda i: (0, i))


SUB_SPEC = pl.BlockSpec((MODES, SUBS, LANES), lambda i: (0, 0, i))


def carries(total, rates, y_hi, z, x):
    width = total.shape[1]
    decay = jnp.exp(-float(ROWS) * rates)
    decay_group = jnp.exp(-float(ROWS * X) * rates)
    slots = jnp.broadcast_to(total.astype(jnp.bfloat16)[None], (Y_HI * X, MODES, width))
    slots = lax.all_to_all(slots, ("y_hi", "x"), 0, 0, tiled=True).astype(jnp.float32)

    def through(y):
        state = slots[X * y]
        for i in range(1, X):
            state = state * decay + slots[X * y + i]
        return state

    ends = [through(y) for y in range(Y_HI)]
    here = jnp.where(y_hi == 0, ends[0], ends[1])
    near = jnp.zeros_like(total)
    for i in range(X - 1):
        slot = jnp.where(y_hi == 0, slots[i], slots[X + i])
        near = jnp.where(i < x, near * decay + slot, near)
    shift = jnp.exp(-rates * (x * ROWS).astype(jnp.float32))
    wrap = jnp.exp(-rates * ((Z - 1 - z) * (ROWS * X)).astype(jnp.float32))
    state = jnp.where(y_hi == 1, wrap * ends[0], 0.0)
    sends = []
    for i in range(Z):
        sends.append((state * shift).astype(jnp.bfloat16))
        state = state * decay_group + jnp.where(z == i, here, 0.0)
    far = lax.all_to_all(jnp.stack(sends), "z", 0, 0, tiled=True).astype(jnp.float32)
    return near + far.sum(axis=0)


def body(pre_gate, post_gate, values, decay_rates, residues, skip_gain, out_weight):
    rows, width = pre_gate.shape
    y_hi, z, x = lax.axis_index("y_hi"), lax.axis_index("z"), lax.axis_index("x")
    y_lo, core = lax.axis_index("y_lo"), lax.axis_index("core")
    tiles = width // LANES
    rates = decay_rates.T
    f32 = functools.partial(jax.ShapeDtypeStruct, dtype=jnp.float32)
    subs, total = pl.pallas_call(
        states_kernel,
        grid=(tiles,),
        in_specs=[column(rows), column(rows), column(MODES)],
        out_specs=[SUB_SPEC, column(MODES)],
        out_shape=[f32((MODES, SUBS, width)), f32((MODES, width))],
        scratch_shapes=[pltpu.VMEM((rows, LANES), jnp.float32)],
        name="states",
    )(pre_gate, values, rates)
    weights = (residues * jnp.sqrt(-jnp.expm1(-2.0 * decay_rates))).T
    local = pl.pallas_call(
        local_kernel,
        grid=(tiles,),
        in_specs=[column(rows), column(rows), column(MODES), column(MODES), column(1), SUB_SPEC],
        out_specs=column(rows),
        out_shape=f32((rows, width)),
        scratch_shapes=[pltpu.VMEM((rows, LANES), jnp.float32), pltpu.VMEM((STEPS, LANES), jnp.float32)],
        cost_estimate=pl.CostEstimate(flops=3 * 10**9, bytes_accessed=3 * 2**20, transcendentals=0),
        name="local",
    )(pre_gate, values, rates, weights, skip_gain[None, :], subs)
    carry = carries(total, rates, y_hi, z, x)
    gated = pl.pallas_call(
        carry_kernel,
        grid=(tiles,),
        in_specs=[column(rows), column(rows), column(MODES), column(MODES), column(MODES)],
        out_specs=column(rows),
        out_shape=jax.ShapeDtypeStruct((rows, width), jnp.bfloat16),
        name="carry",
    )(local, post_gate, rates, weights, carry)

    def block(yl, k):
        return lax.dynamic_slice(out_weight, (0, (yl * CORE + k) * width), (width, width))

    def product(yl, k):
        return jnp.dot(gated, block(yl, k), preferred_element_type=jnp.float32)

    def swap(array, axis):
        return lax.ppermute(array.astype(jnp.bfloat16), axis, [(0, 1), (1, 0)]).astype(jnp.float32)

    far_sum = swap(product(1 - y_lo, 1 - core), "core") + product(1 - y_lo, core)
    far_sum = swap(far_sum, "y_lo")
    near_sum = swap(product(y_lo, 1 - core), "core") + product(y_lo, core)
    return (near_sum + far_sum).astype(jnp.bfloat16)


def solution(mesh):
    axes = ("y_hi", "z", "x", "y_lo", "core")
    split = Mesh(mesh.devices.reshape(Y_HI, Z, X, Y_LO, CORE), axes)
    seq, chan = axes[:3], axes[3:]
    placed = (P(seq, chan), P(seq, chan), P(seq, chan), P(chan, None), P(chan, None), P(chan), P(chan, None))
    return jax.shard_map(body, mesh=split, in_specs=placed, out_specs=P(seq, chan), check_vma=False)
```

```python
import functools

import jax
import jax.numpy as jnp
from jax import lax
from jax.experimental import pallas as pl
from jax.experimental.pallas import tpu as pltpu
from jax.sharding import Mesh
from jax.sharding import PartitionSpec as P

Y_HI, Z, X, Y_LO, CORE = 2, 8, 4, 2, 2
MODES = 16
ROWS = 256
SUBS = 8
STEPS = ROWS // SUBS
LANES = 128
CHUNK = 256
ANY = pl.BlockSpec(memory_space=pl.ANY)
VMEM = pl.BlockSpec(memory_space=pltpu.VMEM)
SMEM = pl.BlockSpec(memory_space=pltpu.SMEM)
PARAMS = pltpu.CompilerParams(vmem_limit_bytes=16 * 2**20)


def in_hbm(array):
    return pltpu.with_memory_space_constraint(array, pltpu.HBM)


def in_vmem(array):
    return pltpu.with_memory_space_constraint(array, pltpu.VMEM)


def shape_of(shape, dtype=jnp.float32):
    return jax.ShapeDtypeStruct(shape, dtype)


def rows8(row):
    return jnp.broadcast_to(row, (SUBS, row.shape[-1]))


def add_all(terms):
    terms = list(terms)
    while len(terms) > 1:
        terms = [a + b for a, b in zip(terms[::2], terms[1::2])] + terms[len(terms) & ~1 :]
    return terms[0]


def inner_of(pre, val):
    product = pre.astype(jnp.float32) * val.astype(jnp.float32)
    return product.astype(jnp.bfloat16).astype(jnp.float32)


def tile_of(index):
    return pl.ds(pl.multiple_of(index * LANES, LANES), LANES)


def states_kernel(pre_hbm, val_hbm, rate_hbm, slots_ref, pre_buf, val_buf, rate_buf, sems):
    width = pre_hbm.shape[1]
    copies = []
    for start in range(0, width, CHUNK):
        part = pl.ds(start, CHUNK)
        n = len(copies)
        copies.append(
            [
                pltpu.make_async_copy(hbm.at[:, part], buf.at[:, part], sems.at[n, j])
                for j, (hbm, buf) in enumerate(((rate_hbm, rate_buf), (pre_hbm, pre_buf), (val_hbm, val_buf)))
            ]
        )
        for copy in copies[-1]:
            copy.start()
    left = (SUBS - 1 - lax.broadcasted_iota(jnp.int32, (SUBS, LANES), 0)).astype(jnp.float32)

    def tile(index):
        cols = tile_of(index)
        factors = [jnp.exp(-float(SUBS) * rows8(rate_buf[m : m + 1, cols])) for m in range(MODES)]
        states = None
        for start in range(0, ROWS, 2 * SUBS):
            rows = pl.ds(start, 2 * SUBS)
            value = inner_of(pre_buf[rows, cols], val_buf[rows, cols])
            for half in (value[:SUBS], value[SUBS:]):
                if states is None:
                    states = [half] * MODES
                else:
                    states = [f * s + half for f, s in zip(factors, states)]
        totals = []
        for m in range(MODES):
            weight = jnp.exp(-rows8(rate_buf[m : m + 1, cols]) * left)
            totals.append(jnp.sum(states[m] * weight, axis=0, keepdims=True))
        total = jnp.concatenate(totals, axis=0).astype(jnp.bfloat16)
        for slot in range(slots_ref.shape[0]):
            slots_ref[slot, :, cols] = total

    for n, group in enumerate(copies):
        for copy in group:
            copy.wait()
        pl.loop(n * (CHUNK // LANES), (n + 1) * (CHUNK // LANES))(tile)


def local_kernel(pre_ref, val_ref, rate_ref, weight_ref, skip_ref, out_ref, inner_buf, taps_buf, sums_buf):
    lag = lax.broadcasted_iota(jnp.int32, (STEPS, LANES), 0).astype(jnp.float32)
    first = lax.broadcasted_iota(jnp.int32, (STEPS, LANES), 0) == 0
    where = lax.broadcasted_iota(jnp.int32, (SUBS, LANES), 0)

    def at(step):
        return inner_buf[pl.ds(step, SUBS, stride=STEPS), :]

    def tile(index):
        cols = tile_of(index)
        inner_buf[...] = inner_of(pre_ref[:, cols], val_ref[:, cols])
        taps = jnp.where(first, skip_ref[:, cols], 0.0)
        for m in range(MODES):
            taps = taps + weight_ref[m : m + 1, cols] * jnp.exp(-rate_ref[m : m + 1, cols] * lag)
        for step in range(STEPS):
            taps_buf[pl.ds(step * SUBS, SUBS), :] = rows8(taps[step : step + 1])
        factors = [jnp.exp(-rows8(rate_ref[m : m + 1, cols])) for m in range(MODES)]
        states = [at(0)] * MODES
        for step in range(1, STEPS):
            value = at(step)
            states = [f * s + value for f, s in zip(factors, states)]
        entering = []
        for m in range(MODES):
            rate = rows8(rate_ref[m : m + 1, cols])
            state = states[m]
            span = 1
            while span < SUBS:
                moved = jnp.where(where >= span, pltpu.roll(state, span, 0), 0.0)
                state = state + jnp.exp(-rate * float(span * STEPS)) * moved
                span *= 2
            state = jnp.where(where >= 1, pltpu.roll(state, 1, 0), 0.0)
            entering.append(state * factors[m] * rows8(weight_ref[m : m + 1, cols]))
        for base in range(0, STEPS, SUBS):
            sums = []
            for _ in range(SUBS):
                sums.append(add_all(entering))
                entering = [f * e for f, e in zip(factors, entering)]
            for source in range(base + SUBS):
                value = at(source)
                for j in range(max(0, source - base), SUBS):
                    tap = taps_buf[pl.ds((base + j - source) * SUBS, SUBS), :]
                    sums[j] = sums[j] + tap * value
            for j in range(SUBS):
                sums_buf[pl.ds(base + j, SUBS, stride=STEPS), :] = sums[j]
        out_ref[:, cols] = sums_buf[...]

    pl.loop(0, out_ref.shape[1] // LANES)(tile)


def spread_kernel(place_ref, slots_ref, rate_ref, near_ref, sends_ref):
    y_hi, z, x = place_ref[0], place_ref[1], place_ref[2]
    shift_rows = (x * ROWS).astype(jnp.float32)
    wrap_rows = ((Z - 1 - z) * (ROWS * X)).astype(jnp.float32)

    def tile(index):
        cols = tile_of(index)
        rate = rate_ref[:, cols]
        decay = jnp.exp(-float(ROWS) * rate)
        slots = [slots_ref[i, :, cols].astype(jnp.float32) for i in range(Y_HI * X)]

        def through(state, rest):
            for slot in rest:
                state = state * decay + slot
            return state

        ends = [through(slots[X * y], slots[X * y + 1 : X * y + X]) for y in range(Y_HI)]
        near = jnp.zeros_like(rate)
        for i in range(X - 1):
            slot = jnp.where(y_hi == 0, slots[i], slots[X + i])
            near = jnp.where(i < x, near * decay + slot, near)
        near_ref[:, cols] = near
        shift = jnp.exp(-rate * shift_rows)
        here = jnp.where(y_hi == 0, ends[0], ends[1]) * shift
        state = jnp.where(y_hi == 1, jnp.exp(-rate * wrap_rows) * ends[0], 0.0) * shift
        decay = jnp.exp(-float(ROWS * X) * rate)
        for i in range(Z):
            sends_ref[i, :, cols] = state.astype(jnp.bfloat16)
            state = state * decay + jnp.where(z == i, here, 0.0)

    pl.loop(0, near_ref.shape[1] // LANES)(tile)


def mix_kernel(
    place_ref, far_ref, near_ref, rate_ref, weight_ref, left_ref, right_ref, post_ref, proj_ref, sent_ref, kept_ref, gated_buf
):
    width = near_ref.shape[1]
    ahead = (lax.broadcasted_iota(jnp.int32, (SUBS, LANES), 0) + 1).astype(jnp.float32)

    def tile(index, local_ref, offset):
        here = tile_of(index)
        cols = tile_of(index + offset)
        carry = near_ref[:, cols] + add_all(far_ref[i, :, cols].astype(jnp.float32) for i in range(Z))
        carry = carry * weight_ref[:, cols]
        terms = []
        factors = []
        for m in range(MODES):
            rate = rows8(rate_ref[m : m + 1, cols])
            terms.append(jnp.exp(-rate * ahead) * rows8(carry[m : m + 1]))
            factors.append(jnp.exp(-rate * float(SUBS)))
        for start in range(0, ROWS, 2 * SUBS):
            sums = []
            for _ in range(2):
                sums.append(add_all(terms))
                terms = [f * t for f, t in zip(factors, terms)]
            rows = pl.ds(start, 2 * SUBS)
            conv = local_ref[rows, here] + jnp.concatenate(sums, axis=0)
            gated_buf[rows, cols] = (post_ref[rows, cols].astype(jnp.float32) * conv).astype(jnp.bfloat16)

    half = left_ref.shape[1] // LANES
    pl.loop(0, half)(lambda i: tile(i, left_ref, 0))
    pl.loop(0, half)(lambda i: tile(i, right_ref, half))
    y_lo, core = place_ref[3], place_ref[4]
    for chip in range(Y_LO):
        for own, out_ref in enumerate((sent_ref, kept_ref)):
            to_chip = 1 - y_lo if chip == 0 else y_lo
            to_core = core if own else 1 - core
            first = (to_chip * CORE + to_core) * width

            def strip(n, first=first, chip=chip, out_ref=out_ref):
                cols = pl.ds(pl.multiple_of(first + n * CHUNK, CHUNK), CHUNK)
                sums = jnp.dot(gated_buf[...], proj_ref[:, cols], preferred_element_type=jnp.float32)
                out_ref[chip, :, pl.ds(pl.multiple_of(n * CHUNK, CHUNK), CHUNK)] = sums.astype(out_ref.dtype)

            pl.loop(0, width // CHUNK)(strip)


def body(pre_gate, post_gate, values, decay_rates, residues, skip_gain, out_weight):
    rows, width = pre_gate.shape
    half = width // 2
    places = [lax.axis_index(name) for name in ("y_hi", "z", "x", "y_lo", "core")]
    place = jnp.stack(places)
    rates = decay_rates.T
    parts = width // CHUNK
    slots = pl.pallas_call(
        states_kernel,
        in_specs=[ANY] * 3,
        out_specs=VMEM,
        out_shape=shape_of((Y_HI * X, MODES, width), jnp.bfloat16),
        scratch_shapes=[
            pltpu.VMEM((rows, width), jnp.bfloat16),
            pltpu.VMEM((rows, width), jnp.bfloat16),
            pltpu.VMEM((MODES, width), jnp.float32),
            pltpu.SemaphoreType.DMA((parts, 3)),
        ],
        name="states",
        compiler_params=PARAMS,
    )(in_hbm(pre_gate), in_hbm(values), in_hbm(rates))
    slots = lax.all_to_all(slots, ("y_hi", "x"), 0, 0, tiled=True)
    weights = (residues * jnp.sqrt(-jnp.expm1(-2.0 * decay_rates))).T

    def local(start, pre, val):
        cols = slice(start, start + half)
        column = pl.BlockSpec((rows, half), lambda i: (0, start // half))
        modes = pl.BlockSpec((MODES, half), lambda i: (0, start // half))
        one = pl.BlockSpec((1, half), lambda i: (0, start // half))
        return pl.pallas_call(
            local_kernel,
            grid=(1,),
            in_specs=[column, column, modes, modes, one],
            out_specs=pl.BlockSpec((rows, half), lambda i: (0, 0)),
            out_shape=shape_of((rows, half)),
            scratch_shapes=[pltpu.VMEM((rows, LANES), jnp.float32)] * 3,
            cost_estimate=pl.CostEstimate(flops=10**8, bytes_accessed=2**20, transcendentals=0),
            name="local",
            compiler_params=PARAMS,
        )(pre, val, rates, weights, skip_gain[None, :])

    left = local(0, pre_gate, values)
    near, sends = pl.pallas_call(
        spread_kernel,
        in_specs=[SMEM, VMEM, VMEM],
        out_specs=[VMEM, VMEM],
        out_shape=[shape_of((MODES, width)), shape_of((Z, MODES, width), jnp.bfloat16)],
        name="spread",
        compiler_params=PARAMS,
    )(place, slots, rates)
    later_pre, later_val, _ = lax.optimization_barrier((pre_gate, values, near))
    right = local(half, later_pre, later_val)
    far = lax.all_to_all(sends, "z", 0, 0, tiled=True)
    sent, kept = pl.pallas_call(
        mix_kernel,
        in_specs=[SMEM] + [VMEM] * 8,
        out_specs=[VMEM, VMEM],
        out_shape=[shape_of((2, rows, width), jnp.bfloat16), shape_of((2, rows, width))],
        scratch_shapes=[pltpu.VMEM((rows, width), jnp.bfloat16)],
        name="mix",
        compiler_params=PARAMS,
    )(place, far, near, rates, weights, in_vmem(left), in_vmem(right), in_vmem(post_gate), in_vmem(out_weight))

    def swap(array, axis):
        return lax.ppermute(array.astype(jnp.bfloat16), axis, [(0, 1), (1, 0)]).astype(jnp.float32)

    far_sum = swap(swap(sent[0], "core") + kept[0], "y_lo")
    near_sum = swap(sent[1], "core") + kept[1]
    return (near_sum + far_sum).astype(jnp.bfloat16)


def solution(mesh):
    axes = ("y_hi", "z", "x", "y_lo", "core")
    split = Mesh(mesh.devices.reshape(Y_HI, Z, X, Y_LO, CORE), axes)
    seq, chan = axes[:3], axes[3:]
    placed = (P(seq, chan), P(seq, chan), P(seq, chan), P(chan, None), P(chan, None), P(chan), P(chan, None))
    return jax.shard_map(body, mesh=split, in_specs=placed, out_specs=P(seq, chan), check_vma=False)
```

```python
import functools

import jax
import jax.numpy as jnp
from jax import lax
from jax.experimental import pallas as pl
from jax.experimental.pallas import tpu as pltpu
from jax.sharding import Mesh
from jax.sharding import PartitionSpec as P

Y_HI, Z, X, Y_LO, CORE = 2, 8, 4, 2, 2
MODES = 16
ROWS = 256
SUBS = 8
STEPS = ROWS // SUBS
LANES = 128
PARTS = 4
CHUNK = 256
ANY = pl.BlockSpec(memory_space=pl.ANY)
VMEM = pl.BlockSpec(memory_space=pltpu.VMEM)
SMEM = pl.BlockSpec(memory_space=pltpu.SMEM)
COST = pl.CostEstimate(flops=2 * 10**9, bytes_accessed=4 * 2**20, transcendentals=0)
PARAMS = pltpu.CompilerParams(vmem_limit_bytes=16 * 2**20)


def in_hbm(array):
    return pltpu.with_memory_space_constraint(array, pltpu.HBM)


def in_vmem(array):
    return pltpu.with_memory_space_constraint(array, pltpu.VMEM)


def shape_of(shape, dtype=jnp.float32):
    return jax.ShapeDtypeStruct(shape, dtype)


def rows8(row):
    return jnp.broadcast_to(row, (SUBS, row.shape[-1]))


def add_all(terms):
    terms = list(terms)
    while len(terms) > 1:
        terms = [a + b for a, b in zip(terms[::2], terms[1::2])] + terms[len(terms) & ~1 :]
    return terms[0]


def tile_of(index):
    return pl.ds(pl.multiple_of(index * LANES, LANES), LANES)


def expm1(value):
    series = jnp.ones_like(value)
    for n in range(9, 1, -1):
        series = 1.0 + value * (1.0 / n) * series
    return jnp.where(jnp.abs(value) < 0.25, value * series, jnp.exp(value) - 1.0)


def states_kernel(
    pre_hbm, val_hbm, rate_hbm, residue_hbm, skip_hbm,
    slots_ref, inner_ref, rate_ref, weight_ref, skip_ref, pre_buf, val_buf, residue_buf, sems
):
    width = pre_hbm.shape[1]
    pairs = ((rate_hbm, rate_ref), (pre_hbm, pre_buf), (val_hbm, val_buf), (residue_hbm, residue_buf), (skip_hbm, skip_ref))
    copies = []
    for start in range(0, width, CHUNK):
        part = pl.ds(start, CHUNK)
        n = len(copies)
        copies.append(
            [pltpu.make_async_copy(hbm.at[:, part], buf.at[:, part], sems.at[n, j]) for j, (hbm, buf) in enumerate(pairs)]
        )
        for copy in copies[-1]:
            copy.start()
    left = (SUBS - 1 - lax.broadcasted_iota(jnp.int32, (SUBS, LANES), 0)).astype(jnp.float32)

    def tile(index):
        cols = tile_of(index)
        factors = [jnp.exp(-float(SUBS) * rows8(rate_ref[m : m + 1, cols])) for m in range(MODES)]
        states = None
        for start in range(0, ROWS, 2 * SUBS):
            rows = pl.ds(start, 2 * SUBS)
            product = pre_buf[rows, cols].astype(jnp.float32) * val_buf[rows, cols].astype(jnp.float32)
            product = product.astype(jnp.bfloat16)
            inner_ref[rows, cols] = product
            value = product.astype(jnp.float32)
            for half in (value[:SUBS], value[SUBS:]):
                if states is None:
                    states = [half] * MODES
                else:
                    states = [f * s + half for f, s in zip(factors, states)]
        totals = []
        for m in range(MODES):
            weight = jnp.exp(-rows8(rate_ref[m : m + 1, cols]) * left)
            totals.append(jnp.sum(states[m] * weight, axis=0, keepdims=True))
        total = jnp.concatenate(totals, axis=0).astype(jnp.bfloat16)
        for slot in range(slots_ref.shape[0]):
            slots_ref[slot, :, cols] = total
        weight_ref[:, cols] = residue_buf[:, cols] * jnp.sqrt(-expm1(-2.0 * rate_ref[:, cols]))

    for n, group in enumerate(copies):
        for copy in group:
            copy.wait()
        pl.loop(n * (CHUNK // LANES), (n + 1) * (CHUNK // LANES))(tile)


def local_kernel(inner_ref, rate_ref, weight_ref, skip_ref, out_ref, inner_buf, taps_buf, sums_buf, *, first_tile):
    lag = lax.broadcasted_iota(jnp.int32, (STEPS, LANES), 0).astype(jnp.float32)
    start = lax.broadcasted_iota(jnp.int32, (STEPS, LANES), 0) == 0
    where = lax.broadcasted_iota(jnp.int32, (SUBS, LANES), 0)

    def at(step):
        return inner_buf[pl.ds(step, SUBS, stride=STEPS), :]

    def tile(index):
        here = tile_of(index)
        cols = tile_of(index + first_tile)
        inner_buf[...] = inner_ref[:, cols].astype(jnp.float32)
        taps = jnp.where(start, skip_ref[:, cols], 0.0)
        for m in range(MODES):
            taps = taps + weight_ref[m : m + 1, cols] * jnp.exp(-rate_ref[m : m + 1, cols] * lag)
        for step in range(STEPS):
            taps_buf[pl.ds(step * SUBS, SUBS), :] = rows8(taps[step : step + 1])
        factors = [jnp.exp(-rows8(rate_ref[m : m + 1, cols])) for m in range(MODES)]
        states = [at(0)] * MODES
        for step in range(1, STEPS):
            value = at(step)
            states = [f * s + value for f, s in zip(factors, states)]
        entering = []
        for m in range(MODES):
            rate = rows8(rate_ref[m : m + 1, cols])
            state = states[m]
            span = 1
            while span < SUBS:
                moved = jnp.where(where >= span, pltpu.roll(state, span, 0), 0.0)
                state = state + jnp.exp(-rate * float(span * STEPS)) * moved
                span *= 2
            state = jnp.where(where >= 1, pltpu.roll(state, 1, 0), 0.0)
            entering.append(state * factors[m] * rows8(weight_ref[m : m + 1, cols]))
        for base in range(0, STEPS, SUBS):
            sums = []
            for _ in range(SUBS):
                sums.append(add_all(entering))
                entering = [f * e for f, e in zip(factors, entering)]
            for source in range(base + SUBS):
                value = at(source)
                for j in range(max(0, source - base), SUBS):
                    tap = taps_buf[pl.ds((base + j - source) * SUBS, SUBS), :]
                    sums[j] = sums[j] + tap * value
            for j in range(SUBS):
                sums_buf[pl.ds(base + j, SUBS, stride=STEPS), :] = sums[j]
        out_ref[:, here] = sums_buf[...]

    pl.loop(0, out_ref.shape[1] // LANES)(tile)


def second_local_kernel(inner_ref, rate_ref, weight_ref, skip_ref, hbm, out_ref, into_ref, *scratch, first_tile):
    *buffers, sem = scratch
    copy = pltpu.make_async_copy(hbm, into_ref, sem)
    copy.start()
    local_kernel(inner_ref, rate_ref, weight_ref, skip_ref, out_ref, *buffers, first_tile=first_tile)
    copy.wait()


def spread_kernel(place_ref, slots_ref, rate_ref, near_ref, sends_ref):
    y_hi, z, x = place_ref[0], place_ref[1], place_ref[2]
    shift_rows = (x * ROWS).astype(jnp.float32)
    wrap_rows = ((Z - 1 - z) * (ROWS * X)).astype(jnp.float32)

    def tile(index):
        cols = tile_of(index)
        rate = rate_ref[:, cols]
        decay = jnp.exp(-float(ROWS) * rate)
        slots = [slots_ref[i, :, cols].astype(jnp.float32) for i in range(Y_HI * X)]

        def through(state, rest):
            for slot in rest:
                state = state * decay + slot
            return state

        ends = [through(slots[X * y], slots[X * y + 1 : X * y + X]) for y in range(Y_HI)]
        near = jnp.zeros_like(rate)
        for i in range(X - 1):
            slot = jnp.where(y_hi == 0, slots[i], slots[X + i])
            near = jnp.where(i < x, near * decay + slot, near)
        near_ref[:, cols] = near
        shift = jnp.exp(-rate * shift_rows)
        here = jnp.where(y_hi == 0, ends[0], ends[1]) * shift
        state = jnp.where(y_hi == 1, jnp.exp(-rate * wrap_rows) * ends[0], 0.0) * shift
        decay = jnp.exp(-float(ROWS * X) * rate)
        for i in range(Z):
            sends_ref[i, :, cols] = state.astype(jnp.bfloat16)
            state = state * decay + jnp.where(z == i, here, 0.0)

    pl.loop(0, near_ref.shape[1] // LANES)(tile)


def fetch(place_ref, proj_hbm, proj_ref, sems, near):
    y_lo, core = place_ref[3], place_ref[4]
    chip = y_lo if near else 1 - y_lo
    width = proj_hbm.shape[0]
    copies = []
    for n, to_core in enumerate((1 - core, core)):
        cols = pl.ds(pl.multiple_of((chip * CORE + to_core) * width, width), width)
        copies.append([])
        for part in range(PARTS):
            rows = pl.ds(part * (width // PARTS), width // PARTS)
            into = proj_ref.at[rows, pl.ds(n * width, width)]
            copies[-1].append(pltpu.make_async_copy(proj_hbm.at[rows, cols], into, sems.at[n, part]))
            copies[-1][-1].start()
    return copies


def mix_kernel(
    place_ref, proj_hbm, far_ref, near_ref, rate_ref, weight_ref, left_ref, right_ref, post_ref, gated_ref, sent_ref, proj_ref, sems
):
    copies = fetch(place_ref, proj_hbm, proj_ref, sems, False)
    rows_count, width = gated_ref.shape
    ahead = (lax.broadcasted_iota(jnp.int32, (SUBS, LANES), 0) + 1).astype(jnp.float32)

    def tile(index, local_ref, offset):
        here = tile_of(index)
        cols = tile_of(index + offset)
        carry = near_ref[:, cols] + add_all(far_ref[i, :, cols].astype(jnp.float32) for i in range(Z))
        carry = carry * weight_ref[:, cols]
        terms = []
        factors = []
        for m in range(MODES):
            rate = rows8(rate_ref[m : m + 1, cols])
            terms.append(jnp.exp(-rate * ahead) * rows8(carry[m : m + 1]))
            factors.append(jnp.exp(-rate * float(SUBS)))
        for start in range(0, rows_count, 2 * SUBS):
            sums = []
            for _ in range(2):
                sums.append(add_all(terms))
                terms = [f * t for f, t in zip(factors, terms)]
            rows = pl.ds(start, 2 * SUBS)
            conv = local_ref[rows, here] + jnp.concatenate(sums, axis=0)
            gated_ref[rows, cols] = (post_ref[rows, cols].astype(jnp.float32) * conv).astype(jnp.bfloat16)

    half = left_ref.shape[1] // LANES
    pl.loop(0, half)(lambda i: tile(i, left_ref, 0))
    pl.loop(0, half)(lambda i: tile(i, right_ref, half))
    arrive(copies[0])
    sums = jnp.dot(gated_ref[...], proj_ref[:, :width], preferred_element_type=jnp.float32)
    sent_ref[...] = sums.astype(sent_ref.dtype)
    arrive(copies[1])


def arrive(copies):
    for copy in copies:
        copy.wait()


def own_kernel(gated_ref, proj_ref, kept_ref):
    width = gated_ref.shape[1]
    kept_ref[...] = jnp.dot(gated_ref[...], proj_ref[:, width:], preferred_element_type=jnp.float32)


def near_kernel(place_ref, proj_hbm, gated_ref, sent_ref, kept_ref, proj_ref, sems):
    copies = fetch(place_ref, proj_hbm, proj_ref, sems, True)
    width = gated_ref.shape[1]
    for n, out_ref in enumerate((sent_ref, kept_ref)):
        arrive(copies[n])
        sums = jnp.dot(gated_ref[...], proj_ref[:, n * width : (n + 1) * width], preferred_element_type=jnp.float32)
        out_ref[...] = sums.astype(out_ref.dtype)


def body(pre_gate, post_gate, values, decay_rates, residues, skip_gain, out_weight):
    rows, width = pre_gate.shape
    half = width // 2
    places = [lax.axis_index(name) for name in ("y_hi", "z", "x", "y_lo", "core")]
    place = jnp.stack(places)
    rates = decay_rates.T
    parts = width // CHUNK
    bf16 = jnp.bfloat16
    slots, inner, rates, weights, skips = pl.pallas_call(
        states_kernel,
        in_specs=[ANY] * 5,
        out_specs=[VMEM] * 5,
        out_shape=[
            shape_of((Y_HI * X, MODES, width), bf16),
            shape_of((rows, width), bf16),
            shape_of((MODES, width)),
            shape_of((MODES, width)),
            shape_of((1, width)),
        ],
        scratch_shapes=[
            pltpu.VMEM((rows, width), bf16),
            pltpu.VMEM((rows, width), bf16),
            pltpu.VMEM((MODES, width), jnp.float32),
            pltpu.SemaphoreType.DMA((parts, 5)),
        ],
        name="states",
        compiler_params=PARAMS,
    )(*(in_hbm(a) for a in (pre_gate, values, decay_rates.T, residues.T, skip_gain[None, :])))
    slots = lax.all_to_all(slots, ("y_hi", "x"), 0, 0, tiled=True)

    def local(start, inner, kernel, more=()):
        return pl.pallas_call(
            functools.partial(kernel, first_tile=start // LANES),
            in_specs=[VMEM] * 4 + [ANY] * len(more),
            out_specs=[VMEM] * (1 + len(more)),
            out_shape=[shape_of((rows, half))] + [shape_of(a.shape, a.dtype) for a in more],
            scratch_shapes=[pltpu.VMEM((rows, LANES), jnp.float32)] * 3 + [pltpu.SemaphoreType.DMA] * len(more),
            cost_estimate=pl.CostEstimate(flops=10**8, bytes_accessed=2**20, transcendentals=0),
            name="local",
            compiler_params=PARAMS,
        )(*(in_vmem(a) for a in (inner, rates, weights, skips)), *(in_hbm(a) for a in more))

    (left,) = local(0, inner, local_kernel)
    slots, left = lax.optimization_barrier((slots, left))
    near, sends = pl.pallas_call(
        spread_kernel,
        in_specs=[SMEM, VMEM, VMEM],
        out_specs=[VMEM, VMEM],
        out_shape=[shape_of((MODES, width)), shape_of((Z, MODES, width), bf16)],
        name="spread",
        compiler_params=PARAMS,
    )(place, in_vmem(slots), in_vmem(rates))
    later_inner, _ = lax.optimization_barrier((inner, near))
    right, post = local(half, later_inner, second_local_kernel, (post_gate,))
    far = lax.all_to_all(sends, "z", 0, 0, tiled=True)
    arrays = tuple(in_vmem(a) for a in (far, near, rates, weights, left, right, post))
    gated, sent, proj_far = pl.pallas_call(
        mix_kernel,
        in_specs=[SMEM, ANY] + [VMEM] * 7,
        out_specs=[VMEM] * 3,
        out_shape=[shape_of((rows, width), bf16), shape_of((rows, width), bf16), shape_of((width, CORE * width), bf16)],
        scratch_shapes=[pltpu.SemaphoreType.DMA((CORE, PARTS))],
        cost_estimate=COST,
        name="mix",
        compiler_params=PARAMS,
    )(place, in_hbm(out_weight), *arrays)
    kept = pl.pallas_call(
        own_kernel,
        in_specs=[VMEM] * 2,
        out_specs=VMEM,
        out_shape=shape_of((rows, width)),
        cost_estimate=COST,
        name="own",
        compiler_params=PARAMS,
    )(in_vmem(gated), in_vmem(proj_far))

    def swap(array, axis):
        return lax.ppermute(array.astype(jnp.bfloat16), axis, [(0, 1), (1, 0)]).astype(jnp.float32)

    to_far = (swap(sent, "core") + kept).astype(bf16)
    gated, to_far = lax.optimization_barrier((gated, to_far))
    far_sum = swap(to_far, "y_lo")
    sent, kept = pl.pallas_call(
        near_kernel,
        in_specs=[SMEM, ANY, VMEM],
        out_specs=[VMEM] * 2,
        out_shape=[shape_of((rows, width), bf16), shape_of((rows, width))],
        scratch_shapes=[pltpu.VMEM((width, CORE * width), bf16), pltpu.SemaphoreType.DMA((CORE, PARTS))],
        cost_estimate=COST,
        name="near",
        compiler_params=PARAMS,
    )(place, in_hbm(out_weight), in_vmem(gated))
    quarter = rows // 4
    received = [swap(sent[i : i + quarter], "core") for i in range(0, rows, quarter)]
    near_sum = jnp.concatenate(received, axis=0) + kept
    return (near_sum + far_sum).astype(bf16)


def solution(mesh):
    axes = ("y_hi", "z", "x", "y_lo", "core")
    split = Mesh(mesh.devices.reshape(Y_HI, Z, X, Y_LO, CORE), axes)
    seq, chan = axes[:3], axes[3:]
    placed = (P(seq, chan), P(seq, chan), P(seq, chan), P(chan, None), P(chan, None), P(chan), P(chan, None))
    return jax.shard_map(body, mesh=split, in_specs=placed, out_specs=P(seq, chan), check_vma=False)
```

```python
import functools

import jax
import jax.numpy as jnp
from jax import lax
from jax.experimental import pallas as pl
from jax.experimental.pallas import tpu as pltpu
from jax.sharding import Mesh
from jax.sharding import PartitionSpec as P

Y_HI, Z, X, Y_LO, CORE = 2, 8, 4, 2, 2
MODES = 16
ROWS = 256
SUBS = 8
STEPS = ROWS // SUBS
LANES = 128
CHUNK = 256
ANY = pl.BlockSpec(memory_space=pl.ANY)
VMEM = pl.BlockSpec(memory_space=pltpu.VMEM)
SMEM = pl.BlockSpec(memory_space=pltpu.SMEM)
EXCHANGES = (("x", X, 1), ("x", X, 3), ("z", Z, 1), ("z", Z, 2), ("z", Z, 6), ("y_hi", Y_HI, 1))
LOCAL_COST = pl.CostEstimate(flops=10**8, bytes_accessed=2**20, transcendentals=0)
COST = pl.CostEstimate(flops=2 * 10**9, bytes_accessed=4 * 2**20, transcendentals=0)
PARAMS = pltpu.CompilerParams(vmem_limit_bytes=16 * 2**20)


def in_hbm(array):
    return pltpu.with_memory_space_constraint(array, pltpu.HBM)


def in_vmem(array):
    return pltpu.with_memory_space_constraint(array, pltpu.VMEM)


def shape_of(shape, dtype=jnp.float32):
    return jax.ShapeDtypeStruct(shape, dtype)


def rows8(row):
    return jnp.broadcast_to(row, (SUBS, row.shape[-1]))


def add_all(terms):
    terms = list(terms)
    while len(terms) > 1:
        terms = [a + b for a, b in zip(terms[::2], terms[1::2])] + terms[len(terms) & ~1 :]
    return terms[0]


def tile_of(index):
    return pl.ds(pl.multiple_of(index * LANES, LANES), LANES)


def expm1(value):
    series = jnp.ones_like(value)
    for n in range(9, 1, -1):
        series = 1.0 + value * (1.0 / n) * series
    return jnp.where(jnp.abs(value) < 0.25, value * series, jnp.exp(value) - 1.0)


def states_kernel(
    pre_hbm, val_hbm, rate_hbm, residue_hbm, skip_hbm,
    total_ref, inner_ref, rate_ref, weight_ref, skip_ref, pre_buf, val_buf, residue_buf, sems
):
    width = pre_hbm.shape[1]
    pairs = ((rate_hbm, rate_ref), (pre_hbm, pre_buf), (val_hbm, val_buf), (residue_hbm, residue_buf), (skip_hbm, skip_ref))
    copies = []
    for start in range(0, width, CHUNK):
        part = pl.ds(start, CHUNK)
        n = len(copies)
        copies.append(
            [pltpu.make_async_copy(hbm.at[:, part], buf.at[:, part], sems.at[n, j]) for j, (hbm, buf) in enumerate(pairs)]
        )
        for copy in copies[-1]:
            copy.start()
    left = (SUBS - 1 - lax.broadcasted_iota(jnp.int32, (SUBS, LANES), 0)).astype(jnp.float32)

    def tile(index):
        cols = tile_of(index)
        factors = [jnp.exp(-float(SUBS) * rows8(rate_ref[m : m + 1, cols])) for m in range(MODES)]
        states = None
        for start in range(0, ROWS, 2 * SUBS):
            rows = pl.ds(start, 2 * SUBS)
            product = pre_buf[rows, cols].astype(jnp.float32) * val_buf[rows, cols].astype(jnp.float32)
            product = product.astype(jnp.bfloat16)
            inner_ref[rows, cols] = product
            value = product.astype(jnp.float32)
            for half in (value[:SUBS], value[SUBS:]):
                if states is None:
                    states = [half] * MODES
                else:
                    states = [f * s + half for f, s in zip(factors, states)]
        totals = []
        for m in range(MODES):
            weight = jnp.exp(-rows8(rate_ref[m : m + 1, cols]) * left)
            totals.append(jnp.sum(states[m] * weight, axis=0, keepdims=True))
        total_ref[:, cols] = jnp.concatenate(totals, axis=0)
        weight_ref[:, cols] = residue_buf[:, cols] * jnp.sqrt(-expm1(-2.0 * rate_ref[:, cols]))

    for n, group in enumerate(copies):
        for copy in group:
            copy.wait()
        pl.loop(n * (CHUNK // LANES), (n + 1) * (CHUNK // LANES))(tile)


def local_kernel(inner_ref, rate_ref, weight_ref, skip_ref, out_ref, inner_buf, taps_buf, sums_buf, *, first_tile):
    lag = lax.broadcasted_iota(jnp.int32, (STEPS, LANES), 0).astype(jnp.float32)
    start = lax.broadcasted_iota(jnp.int32, (STEPS, LANES), 0) == 0
    where = lax.broadcasted_iota(jnp.int32, (SUBS, LANES), 0)

    def at(step):
        return inner_buf[pl.ds(step, SUBS, stride=STEPS), :]

    def tile(index):
        here = tile_of(index)
        cols = tile_of(index + first_tile)
        inner_buf[...] = inner_ref[:, cols].astype(jnp.float32)
        taps = jnp.where(start, skip_ref[:, cols], 0.0)
        for m in range(MODES):
            taps = taps + weight_ref[m : m + 1, cols] * jnp.exp(-rate_ref[m : m + 1, cols] * lag)
        for step in range(STEPS):
            taps_buf[pl.ds(step * SUBS, SUBS), :] = rows8(taps[step : step + 1])
        factors = [jnp.exp(-rows8(rate_ref[m : m + 1, cols])) for m in range(MODES)]
        states = [at(0)] * MODES
        for step in range(1, STEPS):
            value = at(step)
            states = [f * s + value for f, s in zip(factors, states)]
        entering = []
        for m in range(MODES):
            rate = rows8(rate_ref[m : m + 1, cols])
            state = states[m]
            span = 1
            while span < SUBS:
                moved = jnp.where(where >= span, pltpu.roll(state, span, 0), 0.0)
                state = state + jnp.exp(-rate * float(span * STEPS)) * moved
                span *= 2
            state = jnp.where(where >= 1, pltpu.roll(state, 1, 0), 0.0)
            entering.append(state * factors[m] * rows8(weight_ref[m : m + 1, cols]))
        for base in range(0, STEPS, SUBS):
            sums = []
            for _ in range(SUBS):
                sums.append(add_all(entering))
                entering = [f * e for f, e in zip(factors, entering)]
            for source in range(base + SUBS):
                value = at(source)
                for j in range(max(0, source - base), SUBS):
                    tap = taps_buf[pl.ds((base + j - source) * SUBS, SUBS), :]
                    sums[j] = sums[j] + tap * value
            for j in range(SUBS):
                sums_buf[pl.ds(base + j, SUBS, stride=STEPS), :] = sums[j]
        out_ref[:, here] = sums_buf[...]

    pl.loop(0, out_ref.shape[1] // LANES)(tile)


def first_column(place_ref, role, width):
    y_lo, core = place_ref[0], place_ref[1]
    chip = y_lo if role >= CORE else 1 - y_lo
    to_core = core if role % CORE else 1 - core
    return pl.multiple_of((chip * CORE + to_core) * width, width)


def fetching_kernel(place_ref, proj_hbm, post_hbm, inner_ref, rate_ref, weight_ref, skip_ref, out_ref, *refs, first_tile):
    *roles, post_ref, inner_buf, taps_buf, sums_buf, sems = refs
    width, part = roles[0].shape
    cols = pl.ds(first_tile * LANES, part)
    copies = [pltpu.make_async_copy(post_hbm.at[:, cols], post_ref, sems.at[len(roles)])]
    for role, role_ref in enumerate(roles):
        start = pl.multiple_of(first_column(place_ref, role, width) + first_tile * LANES, part)
        copies.append(pltpu.make_async_copy(proj_hbm.at[:, pl.ds(start, part)], role_ref, sems.at[role]))
    for copy in copies:
        copy.start()
    buffers = (inner_buf, taps_buf, sums_buf)
    local_kernel(inner_ref, rate_ref, weight_ref, skip_ref, out_ref, *buffers, first_tile=first_tile)
    for copy in copies:
        copy.wait()


def project(gated_ref, proj_refs, out_ref):
    start = 0
    for proj_ref in proj_refs:
        part = proj_ref.shape[1]
        sums = jnp.dot(gated_ref[...], proj_ref[...], preferred_element_type=jnp.float32)
        out_ref[:, start : start + part] = sums.astype(out_ref.dtype)
        start += part


def mix_kernel(carry_ref, rate_ref, weight_ref, *refs):
    *refs, gated_ref, sent_ref = refs
    parts = len(refs) // 3
    local_refs, post_refs, proj_refs = refs[:parts], refs[parts : 2 * parts], refs[2 * parts :]
    rows_count = gated_ref.shape[0]
    ahead = (lax.broadcasted_iota(jnp.int32, (SUBS, LANES), 0) + 1).astype(jnp.float32)

    def tile(index, local_ref, post_ref, offset):
        here = tile_of(index)
        cols = tile_of(index + offset)
        carry = carry_ref[:, cols] * weight_ref[:, cols]
        terms = []
        factors = []
        for m in range(MODES):
            rate = rows8(rate_ref[m : m + 1, cols])
            terms.append(jnp.exp(-rate * ahead) * rows8(carry[m : m + 1]))
            factors.append(jnp.exp(-rate * float(SUBS)))
        for start in range(0, rows_count, 2 * SUBS):
            sums = []
            for _ in range(2):
                sums.append(add_all(terms))
                terms = [f * t for f, t in zip(factors, terms)]
            rows = pl.ds(start, 2 * SUBS)
            conv = local_ref[rows, here] + jnp.concatenate(sums, axis=0)
            gated_ref[rows, cols] = (post_ref[rows, here].astype(jnp.float32) * conv).astype(jnp.bfloat16)

    each = local_refs[0].shape[1] // LANES
    for part in range(parts):
        sources = (local_refs[part], post_refs[part], part * each)
        pl.loop(0, each)(lambda i, sources=sources: tile(i, *sources))
    project(gated_ref, proj_refs, sent_ref)


def own_kernel(gated_ref, *refs):
    *proj_refs, kept_ref = refs
    project(gated_ref, proj_refs, kept_ref)


def near_kernel(gated_ref, *refs):
    *proj_refs, sent_ref, kept_ref = refs
    parts = len(proj_refs) // 2
    project(gated_ref, proj_refs[:parts], sent_ref)
    project(gated_ref, proj_refs[parts:], kept_ref)


def body(pre_gate, post_gate, values, decay_rates, residues, skip_gain, out_weight):
    rows, width = pre_gate.shape
    y_hi, z, x = (lax.axis_index(name) for name in ("y_hi", "z", "x"))
    place = jnp.stack([lax.axis_index("y_lo"), lax.axis_index("core")])
    block = (y_hi * Z + z) * X + x
    parts = width // CHUNK
    bf16 = jnp.bfloat16
    places = []
    for step in range(len(EXCHANGES)):
        later = (block >> step) & 1
        offset = (block & ((1 << step) - 1)) * ROWS
        places += [later.astype(jnp.float32), (1 - later).astype(jnp.float32), -offset.astype(jnp.float32)]
    pre_gate, place, *places = lax.optimization_barrier((pre_gate, place, *places))
    total, inner, rates, weights, skips = pl.pallas_call(
        states_kernel,
        in_specs=[ANY] * 5,
        out_specs=[VMEM] * 5,
        out_shape=[
            shape_of((MODES, width)),
            shape_of((rows, width), bf16),
            shape_of((MODES, width)),
            shape_of((MODES, width)),
            shape_of((1, width)),
        ],
        scratch_shapes=[
            pltpu.VMEM((rows, width), bf16),
            pltpu.VMEM((rows, width), bf16),
            pltpu.VMEM((MODES, width), jnp.float32),
            pltpu.SemaphoreType.DMA((parts, 5)),
        ],
        name="states",
        compiler_params=PARAMS,
    )(*(in_hbm(a) for a in (pre_gate, values, decay_rates.T, residues.T, skip_gain[None, :])))

    def local(part, inner):
        outs = [shape_of((rows, CHUNK))] + [shape_of((width, CHUNK), bf16)] * (2 * CORE) + [shape_of((rows, CHUNK), bf16)]
        return pl.pallas_call(
            functools.partial(fetching_kernel, first_tile=part * (CHUNK // LANES)),
            in_specs=[SMEM, ANY, ANY] + [VMEM] * 4,
            out_specs=[VMEM] * len(outs),
            out_shape=outs,
            scratch_shapes=[pltpu.VMEM((rows, LANES), jnp.float32)] * 3 + [pltpu.SemaphoreType.DMA((len(outs),))],
            cost_estimate=LOCAL_COST,
            name="local",
            compiler_params=PARAMS,
        )(place, in_hbm(out_weight), in_hbm(post_gate), *(in_vmem(a) for a in (inner, rates, weights, skips)))

    group = total
    carry = jnp.zeros_like(total)
    pieces = []
    for step, (axis, size, flip) in enumerate(EXCHANGES):
        pairs = [(i, i ^ flip) for i in range(size)]
        other = lax.ppermute(group.astype(bf16), axis, pairs).astype(jnp.float32)
        later, earlier, offset = places[3 * step : 3 * step + 3]
        decay = jnp.exp(-float(ROWS << step) * rates)
        carry = carry + later * jnp.exp(offset * rates) * other
        group = (later * other + earlier * group) * decay + (later * group + earlier * other)
        part = step - (len(EXCHANGES) - parts)
        if part >= 0:
            piece = local(part, inner)
            group, carry, *piece = lax.optimization_barrier((group, carry, *piece))
            pieces.append(piece)
        inner, group, carry = lax.optimization_barrier((inner, group, carry))
    locals_, *roles, posts = (list(part) for part in zip(*pieces))
    arrays = (carry, rates, weights, *locals_, *posts, *roles[0])
    gated, sent = pl.pallas_call(
        mix_kernel,
        in_specs=[VMEM] * len(arrays),
        out_specs=[VMEM] * 2,
        out_shape=[shape_of((rows, width), bf16), shape_of((rows, width), bf16)],
        cost_estimate=COST,
        name="mix",
        compiler_params=PARAMS,
    )(*(in_vmem(a) for a in arrays))
    kept = pl.pallas_call(
        own_kernel,
        in_specs=[VMEM] * (1 + parts),
        out_specs=VMEM,
        out_shape=shape_of((rows, width)),
        cost_estimate=COST,
        name="own",
        compiler_params=PARAMS,
    )(*(in_vmem(a) for a in (gated, *roles[1])))

    def swap(array, axis):
        return lax.ppermute(array.astype(jnp.bfloat16), axis, [(0, 1), (1, 0)]).astype(jnp.float32)

    to_far = (swap(sent, "core") + kept).astype(bf16)
    gated, to_far = lax.optimization_barrier((gated, to_far))
    far_sum = swap(to_far, "y_lo")
    sent, kept = pl.pallas_call(
        near_kernel,
        in_specs=[VMEM] * (1 + 2 * parts),
        out_specs=[VMEM] * 2,
        out_shape=[shape_of((rows, width), bf16), shape_of((rows, width))],
        cost_estimate=COST,
        name="near",
        compiler_params=PARAMS,
    )(*(in_vmem(a) for a in (gated, *roles[2], *roles[3])))
    quarter = rows // 4
    received = [swap(sent[i : i + quarter], "core") for i in range(0, rows, quarter)]
    near_sum = jnp.concatenate(received, axis=0) + kept
    return (near_sum + far_sum).astype(bf16)


def solution(mesh):
    axes = ("y_hi", "z", "x", "y_lo", "core")
    split = Mesh(mesh.devices.reshape(Y_HI, Z, X, Y_LO, CORE), axes)
    seq, chan = axes[:3], axes[3:]
    placed = (P(seq, chan), P(seq, chan), P(seq, chan), P(chan, None), P(chan, None), P(chan), P(chan, None))
    return jax.shard_map(body, mesh=split, in_specs=placed, out_specs=P(seq, chan), check_vma=False)
```

```python
import functools

import jax
import jax.numpy as jnp
from jax import lax
from jax.experimental import pallas as pl
from jax.experimental.pallas import tpu as pltpu
from jax.sharding import Mesh
from jax.sharding import PartitionSpec as P

Y_HI, Z, X, Y_LO, CORE = 2, 8, 4, 2, 2
MODES = 16
ROWS = 256
SUBS = 8
STEPS = ROWS // SUBS
LANES = 128
CHUNK = 256
ANY = pl.BlockSpec(memory_space=pl.ANY)
VMEM = pl.BlockSpec(memory_space=pltpu.VMEM)
SMEM = pl.BlockSpec(memory_space=pltpu.SMEM)
STAGES = (
    ("x", X, ((1, 1), (3, 3), (2, 2))),
    ("z", Z, ((1, 1), (2, 2), (3, 3))),
    ("z", Z, ((6, 1),)),
    ("y_hi", Y_HI, ((1, 1),)),
)
LOCAL_COST = pl.CostEstimate(flops=10**8, bytes_accessed=2**20, transcendentals=0)
COST = pl.CostEstimate(flops=2 * 10**9, bytes_accessed=4 * 2**20, transcendentals=0)
PARAMS = pltpu.CompilerParams(vmem_limit_bytes=16 * 2**20)


def in_hbm(array):
    return pltpu.with_memory_space_constraint(array, pltpu.HBM)


def in_vmem(array):
    return pltpu.with_memory_space_constraint(array, pltpu.VMEM)


def shape_of(shape, dtype=jnp.float32):
    return jax.ShapeDtypeStruct(shape, dtype)


def rows8(row):
    return jnp.broadcast_to(row, (SUBS, row.shape[-1]))


def add_all(terms):
    terms = list(terms)
    while len(terms) > 1:
        terms = [a + b for a, b in zip(terms[::2], terms[1::2])] + terms[len(terms) & ~1 :]
    return terms[0]


def tile_of(index):
    return pl.ds(pl.multiple_of(index * LANES, LANES), LANES)


def expm1(value):
    series = jnp.ones_like(value)
    for n in range(9, 1, -1):
        series = 1.0 + value * (1.0 / n) * series
    return jnp.where(jnp.abs(value) < 0.25, value * series, jnp.exp(value) - 1.0)


def states_kernel(
    pre_hbm, val_hbm, rate_hbm, residue_hbm, skip_hbm,
    total_ref, inner_ref, rate_ref, weight_ref, skip_ref, pre_buf, val_buf, residue_buf, sems
):
    width = pre_hbm.shape[1]
    pairs = ((rate_hbm, rate_ref), (pre_hbm, pre_buf), (val_hbm, val_buf), (residue_hbm, residue_buf), (skip_hbm, skip_ref))
    copies = []
    for start in range(0, width, CHUNK):
        part = pl.ds(start, CHUNK)
        n = len(copies)
        copies.append(
            [pltpu.make_async_copy(hbm.at[:, part], buf.at[:, part], sems.at[n, j]) for j, (hbm, buf) in enumerate(pairs)]
        )
        for copy in copies[-1]:
            copy.start()
    left = (SUBS - 1 - lax.broadcasted_iota(jnp.int32, (SUBS, LANES), 0)).astype(jnp.float32)

    def tile(index):
        cols = tile_of(index)
        factors = [jnp.exp(-float(SUBS) * rows8(rate_ref[m : m + 1, cols])) for m in range(MODES)]
        states = None
        for start in range(0, ROWS, 2 * SUBS):
            rows = pl.ds(start, 2 * SUBS)
            product = pre_buf[rows, cols].astype(jnp.float32) * val_buf[rows, cols].astype(jnp.float32)
            product = product.astype(jnp.bfloat16)
            inner_ref[rows, cols] = product
            value = product.astype(jnp.float32)
            for half in (value[:SUBS], value[SUBS:]):
                if states is None:
                    states = [half] * MODES
                else:
                    states = [f * s + half for f, s in zip(factors, states)]
        totals = []
        for m in range(MODES):
            weight = jnp.exp(-rows8(rate_ref[m : m + 1, cols]) * left)
            totals.append(jnp.sum(states[m] * weight, axis=0, keepdims=True))
        total_ref[:, cols] = jnp.concatenate(totals, axis=0)
        weight_ref[:, cols] = residue_buf[:, cols] * jnp.sqrt(-expm1(-2.0 * rate_ref[:, cols]))

    for n, group in enumerate(copies):
        for copy in group:
            copy.wait()
        pl.loop(n * (CHUNK // LANES), (n + 1) * (CHUNK // LANES))(tile)


def local_kernel(inner_ref, rate_ref, weight_ref, skip_ref, out_ref, inner_buf, taps_buf, sums_buf, *, first_tile):
    lag = lax.broadcasted_iota(jnp.int32, (STEPS, LANES), 0).astype(jnp.float32)
    start = lax.broadcasted_iota(jnp.int32, (STEPS, LANES), 0) == 0
    where = lax.broadcasted_iota(jnp.int32, (SUBS, LANES), 0)

    def at(step):
        return inner_buf[pl.ds(step, SUBS, stride=STEPS), :]

    def tile(index):
        here = tile_of(index)
        cols = tile_of(index + first_tile)
        inner_buf[...] = inner_ref[:, cols].astype(jnp.float32)
        taps = jnp.where(start, skip_ref[:, cols], 0.0)
        for m in range(MODES):
            taps = taps + weight_ref[m : m + 1, cols] * jnp.exp(-rate_ref[m : m + 1, cols] * lag)
        for step in range(STEPS):
            taps_buf[pl.ds(step * SUBS, SUBS), :] = rows8(taps[step : step + 1])
        factors = [jnp.exp(-rows8(rate_ref[m : m + 1, cols])) for m in range(MODES)]
        states = [at(0)] * MODES
        for step in range(1, STEPS):
            value = at(step)
            states = [f * s + value for f, s in zip(factors, states)]
        entering = []
        for m in range(MODES):
            rate = rows8(rate_ref[m : m + 1, cols])
            state = states[m]
            span = 1
            while span < SUBS:
                moved = jnp.where(where >= span, pltpu.roll(state, span, 0), 0.0)
                state = state + jnp.exp(-rate * float(span * STEPS)) * moved
                span *= 2
            state = jnp.where(where >= 1, pltpu.roll(state, 1, 0), 0.0)
            entering.append(state * factors[m] * rows8(weight_ref[m : m + 1, cols]))
        for base in range(0, STEPS, SUBS):
            sums = []
            for _ in range(SUBS):
                sums.append(add_all(entering))
                entering = [f * e for f, e in zip(factors, entering)]
            for source in range(base + SUBS):
                value = at(source)
                for j in range(max(0, source - base), SUBS):
                    tap = taps_buf[pl.ds((base + j - source) * SUBS, SUBS), :]
                    sums[j] = sums[j] + tap * value
            for j in range(SUBS):
                sums_buf[pl.ds(base + j, SUBS, stride=STEPS), :] = sums[j]
        out_ref[:, here] = sums_buf[...]

    pl.loop(0, out_ref.shape[1] // LANES)(tile)


def first_column(place_ref, role, width):
    y_lo, core = place_ref[0], place_ref[1]
    chip = y_lo if role >= CORE else 1 - y_lo
    to_core = core if role % CORE else 1 - core
    return pl.multiple_of((chip * CORE + to_core) * width, width)


def fetching_kernel(place_ref, proj_hbm, post_hbm, inner_ref, rate_ref, weight_ref, skip_ref, out_ref, *refs, first_tile):
    *roles, post_ref, inner_buf, taps_buf, sums_buf, sems = refs
    width, part = roles[0].shape
    cols = pl.ds(first_tile * LANES, part)
    copies = [pltpu.make_async_copy(post_hbm.at[:, cols], post_ref, sems.at[len(roles)])]
    for role, role_ref in enumerate(roles):
        start = pl.multiple_of(first_column(place_ref, role, width) + first_tile * LANES, part)
        copies.append(pltpu.make_async_copy(proj_hbm.at[:, pl.ds(start, part)], role_ref, sems.at[role]))
    for copy in copies:
        copy.start()
    buffers = (inner_buf, taps_buf, sums_buf)
    local_kernel(inner_ref, rate_ref, weight_ref, skip_ref, out_ref, *buffers, first_tile=first_tile)
    for copy in copies:
        copy.wait()


def project(gated_ref, proj_refs, out_ref):
    start = 0
    for proj_ref in proj_refs:
        part = proj_ref.shape[1]
        sums = jnp.dot(gated_ref[...], proj_ref[...], preferred_element_type=jnp.float32)
        out_ref[:, start : start + part] = sums.astype(out_ref.dtype)
        start += part


def mix_kernel(carry_ref, rate_ref, weight_ref, *refs):
    *refs, gated_ref, sent_ref = refs
    parts = len(refs) // 3
    local_refs, post_refs, proj_refs = refs[:parts], refs[parts : 2 * parts], refs[2 * parts :]
    rows_count = gated_ref.shape[0]
    ahead = (lax.broadcasted_iota(jnp.int32, (SUBS, LANES), 0) + 1).astype(jnp.float32)

    def tile(index, local_ref, post_ref, offset):
        here = tile_of(index)
        cols = tile_of(index + offset)
        carry = carry_ref[:, cols] * weight_ref[:, cols]
        terms = []
        factors = []
        for m in range(MODES):
            rate = rows8(rate_ref[m : m + 1, cols])
            terms.append(jnp.exp(-rate * ahead) * rows8(carry[m : m + 1]))
            factors.append(jnp.exp(-rate * float(SUBS)))
        for start in range(0, rows_count, 2 * SUBS):
            sums = []
            for _ in range(2):
                sums.append(add_all(terms))
                terms = [f * t for f, t in zip(factors, terms)]
            rows = pl.ds(start, 2 * SUBS)
            conv = local_ref[rows, here] + jnp.concatenate(sums, axis=0)
            gated_ref[rows, cols] = (post_ref[rows, here].astype(jnp.float32) * conv).astype(jnp.bfloat16)

    each = local_refs[0].shape[1] // LANES
    for part in range(parts):
        sources = (local_refs[part], post_refs[part], part * each)
        pl.loop(0, each)(lambda i, sources=sources: tile(i, *sources))
    project(gated_ref, proj_refs, sent_ref)


def own_kernel(gated_ref, *refs):
    *proj_refs, kept_ref = refs
    project(gated_ref, proj_refs, kept_ref)


def near_kernel(gated_ref, *refs):
    *proj_refs, sent_ref, kept_ref = refs
    parts = len(proj_refs) // 2
    project(gated_ref, proj_refs[:parts], sent_ref)
    project(gated_ref, proj_refs[parts:], kept_ref)


def body(pre_gate, post_gate, values, decay_rates, residues, skip_gain, out_weight):
    rows, width = pre_gate.shape
    y_hi, z, x = (lax.axis_index(name) for name in ("y_hi", "z", "x"))
    place = jnp.stack([lax.axis_index("y_lo"), lax.axis_index("core")])
    block = (y_hi * Z + z) * X + x
    parts = width // CHUNK
    bf16 = jnp.bfloat16
    places = []
    blocks = 1
    for _, _, partners in STAGES:
        ways = len(partners) + 1
        mine = block // blocks % ways
        for other in (0,) + tuple(other for _, other in partners):
            member = mine ^ other
            after = (ways - 1 - member) * (blocks * ROWS)
            before = (mine - 1 - member) * (blocks * ROWS) + block % blocks * ROWS
            places += [-after.astype(jnp.float32), -jnp.maximum(before, 0).astype(jnp.float32), (member < mine).astype(jnp.float32)]
        blocks *= ways
    pre_gate, place, *places = lax.optimization_barrier((pre_gate, place, *places))
    total, inner, rates, weights, skips = pl.pallas_call(
        states_kernel,
        in_specs=[ANY] * 5,
        out_specs=[VMEM] * 5,
        out_shape=[
            shape_of((MODES, width)),
            shape_of((rows, width), bf16),
            shape_of((MODES, width)),
            shape_of((MODES, width)),
            shape_of((1, width)),
        ],
        scratch_shapes=[
            pltpu.VMEM((rows, width), bf16),
            pltpu.VMEM((rows, width), bf16),
            pltpu.VMEM((MODES, width), jnp.float32),
            pltpu.SemaphoreType.DMA((parts, 5)),
        ],
        name="states",
        compiler_params=PARAMS,
    )(*(in_hbm(a) for a in (pre_gate, values, decay_rates.T, residues.T, skip_gain[None, :])))

    def local(part, inner):
        outs = [shape_of((rows, CHUNK))] + [shape_of((width, CHUNK), bf16)] * (2 * CORE) + [shape_of((rows, CHUNK), bf16)]
        return pl.pallas_call(
            functools.partial(fetching_kernel, first_tile=part * (CHUNK // LANES)),
            in_specs=[SMEM, ANY, ANY] + [VMEM] * 4,
            out_specs=[VMEM] * len(outs),
            out_shape=outs,
            scratch_shapes=[pltpu.VMEM((rows, LANES), jnp.float32)] * 3 + [pltpu.SemaphoreType.DMA((len(outs),))],
            cost_estimate=LOCAL_COST,
            name="local",
            compiler_params=PARAMS,
        )(place, in_hbm(out_weight), in_hbm(post_gate), *(in_vmem(a) for a in (inner, rates, weights, skips)))

    group = total
    carry = jnp.zeros_like(total)
    pieces = []
    for step, (axis, size, partners) in enumerate(STAGES):
        others = [
            lax.ppermute(group.astype(bf16), axis, [(i, i ^ flip) for i in range(size)]).astype(jnp.float32)
            for flip, _ in partners
        ]
        after, _, _ = places[:3]
        group = jnp.exp(after * rates) * group
        for n, other in enumerate(others):
            after, before, earlier = places[3 * n + 3 : 3 * n + 6]
            group = group + jnp.exp(after * rates) * other
            carry = carry + earlier * jnp.exp(before * rates) * other
        places = places[3 * len(others) + 3 :]
        part = step - (len(STAGES) - parts)
        if part >= 0:
            piece = local(part, inner)
            group, carry, *piece = lax.optimization_barrier((group, carry, *piece))
            pieces.append(piece)
        inner, group, carry = lax.optimization_barrier((inner, group, carry))
    locals_, *roles, posts = (list(part) for part in zip(*pieces))
    arrays = (carry, rates, weights, *locals_, *posts, *roles[0])
    gated, sent = pl.pallas_call(
        mix_kernel,
        in_specs=[VMEM] * len(arrays),
        out_specs=[VMEM] * 2,
        out_shape=[shape_of((rows, width), bf16), shape_of((rows, width), bf16)],
        cost_estimate=COST,
        name="mix",
        compiler_params=PARAMS,
    )(*(in_vmem(a) for a in arrays))
    kept = pl.pallas_call(
        own_kernel,
        in_specs=[VMEM] * (1 + parts),
        out_specs=VMEM,
        out_shape=shape_of((rows, width)),
        cost_estimate=COST,
        name="own",
        compiler_params=PARAMS,
    )(*(in_vmem(a) for a in (gated, *roles[1])))

    def swap(array, axis):
        return lax.ppermute(array.astype(jnp.bfloat16), axis, [(0, 1), (1, 0)]).astype(jnp.float32)

    to_far = (swap(sent, "core") + kept).astype(bf16)
    gated, to_far = lax.optimization_barrier((gated, to_far))
    far_sum = swap(to_far, "y_lo")
    sent, kept = pl.pallas_call(
        near_kernel,
        in_specs=[VMEM] * (1 + 2 * parts),
        out_specs=[VMEM] * 2,
        out_shape=[shape_of((rows, width), bf16), shape_of((rows, width))],
        cost_estimate=COST,
        name="near",
        compiler_params=PARAMS,
    )(*(in_vmem(a) for a in (gated, *roles[2], *roles[3])))
    quarter = rows // 4
    received = [swap(sent[i : i + quarter], "core") for i in range(0, rows, quarter)]
    near_sum = jnp.concatenate(received, axis=0) + kept
    return (near_sum + far_sum).astype(bf16)


def solution(mesh):
    axes = ("y_hi", "z", "x", "y_lo", "core")
    split = Mesh(mesh.devices.reshape(Y_HI, Z, X, Y_LO, CORE), axes)
    seq, chan = axes[:3], axes[3:]
    placed = (P(seq, chan), P(seq, chan), P(seq, chan), P(chan, None), P(chan, None), P(chan), P(chan, None))
    return jax.shard_map(body, mesh=split, in_specs=placed, out_specs=P(seq, chan), check_vma=False)
```

```python
import functools

import jax
import jax.numpy as jnp
from jax import lax
from jax.experimental import pallas as pl
from jax.experimental.pallas import tpu as pltpu
from jax.sharding import Mesh
from jax.sharding import PartitionSpec as P

Y_HI, Z, X, Y_LO, CORE = 2, 8, 4, 2, 2
MODES = 16
ROWS = 256
SUBS = 8
STEPS = ROWS // SUBS
LANES = 128
CHUNK = 256
ANY = pl.BlockSpec(memory_space=pl.ANY)
VMEM = pl.BlockSpec(memory_space=pltpu.VMEM)
SMEM = pl.BlockSpec(memory_space=pltpu.SMEM)
STAGES = (
    ("x", X, ((1, 1), (3, 3), (2, 2))),
    ("z", Z, ((1, 1), (3, 3), (2, 2))),
    ("z", Z, ((6, 1),)),
    ("y_hi", Y_HI, ((1, 1),)),
)
LOCAL_COST = pl.CostEstimate(flops=10**8, bytes_accessed=2**20, transcendentals=0)
COST = pl.CostEstimate(flops=2 * 10**9, bytes_accessed=4 * 2**20, transcendentals=0)
PARAMS = pltpu.CompilerParams(vmem_limit_bytes=16 * 2**20)


def in_hbm(array):
    return pltpu.with_memory_space_constraint(array, pltpu.HBM)


def in_vmem(array):
    return pltpu.with_memory_space_constraint(array, pltpu.VMEM)


def shape_of(shape, dtype=jnp.float32):
    return jax.ShapeDtypeStruct(shape, dtype)


def rows8(row):
    return jnp.broadcast_to(row, (SUBS, row.shape[-1]))


def add_all(terms):
    terms = list(terms)
    while len(terms) > 1:
        terms = [a + b for a, b in zip(terms[::2], terms[1::2])] + terms[len(terms) & ~1 :]
    return terms[0]


def tile_of(index):
    if isinstance(index, int):
        return pl.ds(index * LANES, LANES)
    return pl.ds(pl.multiple_of(index * LANES, LANES), LANES)


def expm1(value):
    series = jnp.ones_like(value)
    for n in range(9, 1, -1):
        series = 1.0 + value * (1.0 / n) * series
    return jnp.where(jnp.abs(value) < 0.25, value * series, jnp.exp(value) - 1.0)


def states_kernel(
    pre_hbm, val_hbm, rate_hbm, residue_hbm, skip_hbm,
    total_ref, inner_ref, rate_ref, weight_ref, skip_ref, pre_buf, val_buf, residue_buf, sems
):
    width = pre_hbm.shape[1]
    pairs = ((rate_hbm, rate_ref), (pre_hbm, pre_buf), (val_hbm, val_buf), (residue_hbm, residue_buf), (skip_hbm, skip_ref))
    copies = []
    for start in range(0, width, CHUNK):
        part = pl.ds(start, CHUNK)
        n = len(copies)
        copies.append(
            [pltpu.make_async_copy(hbm.at[:, part], buf.at[:, part], sems.at[n, j]) for j, (hbm, buf) in enumerate(pairs)]
        )
        for copy in copies[-1]:
            copy.start()
    left = (SUBS - 1 - lax.broadcasted_iota(jnp.int32, (SUBS, LANES), 0)).astype(jnp.float32)

    def tile(index):
        cols = tile_of(index)
        factors = [jnp.exp(-float(SUBS) * rows8(rate_ref[m : m + 1, cols])) for m in range(MODES)]
        states = None
        for start in range(0, ROWS, 2 * SUBS):
            rows = pl.ds(start, 2 * SUBS)
            product = pre_buf[rows, cols].astype(jnp.float32) * val_buf[rows, cols].astype(jnp.float32)
            product = product.astype(jnp.bfloat16)
            inner_ref[rows, cols] = product
            value = product.astype(jnp.float32)
            for half in (value[:SUBS], value[SUBS:]):
                if states is None:
                    states = [half] * MODES
                else:
                    states = [f * s + half for f, s in zip(factors, states)]
        totals = []
        for m in range(MODES):
            weight = jnp.exp(-rows8(rate_ref[m : m + 1, cols]) * left)
            totals.append(jnp.sum(states[m] * weight, axis=0, keepdims=True))
        total_ref[:, cols] = jnp.concatenate(totals, axis=0)
        weight_ref[:, cols] = residue_buf[:, cols] * jnp.sqrt(-expm1(-2.0 * rate_ref[:, cols]))

    for n, group in enumerate(copies):
        for copy in group:
            copy.wait()
        pl.loop(n * (CHUNK // LANES), (n + 1) * (CHUNK // LANES))(tile)


def local_kernel(inner_ref, rate_ref, weight_ref, skip_ref, out_ref, inner_buf, taps_buf, sums_buf, *, first_tile):
    lag = lax.broadcasted_iota(jnp.int32, (STEPS, LANES), 0).astype(jnp.float32)
    start = lax.broadcasted_iota(jnp.int32, (STEPS, LANES), 0) == 0
    where = lax.broadcasted_iota(jnp.int32, (SUBS, LANES), 0)

    def at(step):
        return inner_buf[pl.ds(step, SUBS, stride=STEPS), :]

    def tile(index):
        here = tile_of(index)
        cols = tile_of(index + first_tile)
        inner_buf[...] = inner_ref[:, cols].astype(jnp.float32)
        taps = jnp.where(start, skip_ref[:, cols], 0.0)
        for m in range(MODES):
            taps = taps + weight_ref[m : m + 1, cols] * jnp.exp(-rate_ref[m : m + 1, cols] * lag)
        for step in range(STEPS):
            taps_buf[pl.ds(step * SUBS, SUBS), :] = rows8(taps[step : step + 1])
        factors = [jnp.exp(-rows8(rate_ref[m : m + 1, cols])) for m in range(MODES)]
        states = [at(0)] * MODES
        for step in range(1, STEPS):
            value = at(step)
            states = [f * s + value for f, s in zip(factors, states)]
        entering = []
        for m in range(MODES):
            rate = rows8(rate_ref[m : m + 1, cols])
            state = states[m]
            span = 1
            while span < SUBS:
                moved = jnp.where(where >= span, pltpu.roll(state, span, 0), 0.0)
                state = state + jnp.exp(-rate * float(span * STEPS)) * moved
                span *= 2
            state = jnp.where(where >= 1, pltpu.roll(state, 1, 0), 0.0)
            entering.append(state * factors[m] * rows8(weight_ref[m : m + 1, cols]))
        for base in range(0, STEPS, SUBS):
            sums = []
            for _ in range(SUBS):
                sums.append(add_all(entering))
                entering = [f * e for f, e in zip(factors, entering)]
            for source in range(base + SUBS):
                value = at(source)
                for j in range(max(0, source - base), SUBS):
                    tap = taps_buf[pl.ds((base + j - source) * SUBS, SUBS), :]
                    sums[j] = sums[j] + tap * value
            for j in range(SUBS):
                sums_buf[pl.ds(base + j, SUBS, stride=STEPS), :] = sums[j]
        out_ref[:, here] = sums_buf[...]

    pl.loop(0, out_ref.shape[1] // LANES)(tile)


def first_column(place_ref, role, width):
    y_lo, core = place_ref[0], place_ref[1]
    chip = y_lo if role >= CORE else 1 - y_lo
    to_core = core if role % CORE else 1 - core
    return pl.multiple_of((chip * CORE + to_core) * width, width)


def fetching_kernel(place_ref, proj_hbm, post_hbm, inner_ref, rate_ref, weight_ref, skip_ref, out_ref, *refs, first_tile):
    *roles, post_ref, inner_buf, taps_buf, sums_buf, sems = refs
    width, part = roles[0].shape
    cols = pl.ds(first_tile * LANES, part)
    copies = [pltpu.make_async_copy(post_hbm.at[:, cols], post_ref, sems.at[len(roles)])]
    for role, role_ref in enumerate(roles):
        start = pl.multiple_of(first_column(place_ref, role, width) + first_tile * LANES, part)
        copies.append(pltpu.make_async_copy(proj_hbm.at[:, pl.ds(start, part)], role_ref, sems.at[role]))
    for copy in copies:
        copy.start()
    buffers = (inner_buf, taps_buf, sums_buf)
    local_kernel(inner_ref, rate_ref, weight_ref, skip_ref, out_ref, *buffers, first_tile=first_tile)
    for copy in copies:
        copy.wait()


def project(gated_ref, proj_refs, out_ref):
    start = 0
    for proj_ref in proj_refs:
        part = proj_ref.shape[1]
        sums = jnp.dot(gated_ref[...], proj_ref[...], preferred_element_type=jnp.float32)
        out_ref[:, start : start + part] = sums.astype(out_ref.dtype)
        start += part


def mix_kernel(carry_ref, rate_ref, weight_ref, *refs):
    *refs, gated_ref, sent_ref, sums_buf = refs
    parts = len(refs) // 3
    local_refs, post_refs, proj_refs = refs[:parts], refs[parts : 2 * parts], refs[2 * parts :]
    rows_count = gated_ref.shape[0]
    ahead = (lax.broadcasted_iota(jnp.int32, (SUBS, LANES), 0) + 1).astype(jnp.float32)

    def tile(index, local_ref, post_ref, offset):
        here = tile_of(index)
        cols = tile_of(index + offset)
        carry = carry_ref[:, cols] * weight_ref[:, cols]
        terms = []
        factors = []
        for m in range(MODES):
            rate = rows8(rate_ref[m : m + 1, cols])
            terms.append(jnp.exp(-rate * ahead) * rows8(carry[m : m + 1]))
            factors.append(jnp.exp(-rate * float(SUBS)))
        for start in range(0, rows_count, 2 * SUBS):
            sums = []
            for _ in range(2):
                sums.append(add_all(terms))
                terms = [f * t for f, t in zip(factors, terms)]
            rows = pl.ds(start, 2 * SUBS)
            conv = local_ref[rows, here] + jnp.concatenate(sums, axis=0)
            gated_ref[rows, cols] = (post_ref[rows, here].astype(jnp.float32) * conv).astype(jnp.bfloat16)

    each = local_refs[0].shape[1] // LANES
    deep = each * LANES

    def add_product(part):
        cols = slice(part * deep, (part + 1) * deep)
        gated = gated_ref[:, cols]
        for n, proj_ref in enumerate(proj_refs):
            into = slice(n * proj_ref.shape[1], (n + 1) * proj_ref.shape[1])
            sums = jnp.dot(gated, proj_ref[cols, :], preferred_element_type=jnp.float32)
            if part:
                sums = sums + sums_buf[:, into]
            if part < parts - 1:
                sums_buf[:, into] = sums
            else:
                sent_ref[:, into] = sums.astype(sent_ref.dtype)

    for part in range(parts):
        if part:
            add_product(part - 1)
        for i in range(each):
            tile(i, local_refs[part], post_refs[part], part * each)
    add_product(parts - 1)


def own_kernel(gated_ref, *refs):
    *proj_refs, kept_ref = refs
    project(gated_ref, proj_refs, kept_ref)


def near_kernel(gated_ref, *refs):
    *proj_refs, sent_ref, kept_ref = refs
    parts = len(proj_refs) // 2
    project(gated_ref, proj_refs[:parts], sent_ref)
    project(gated_ref, proj_refs[parts:], kept_ref)


def body(pre_gate, post_gate, values, decay_rates, residues, skip_gain, out_weight):
    rows, width = pre_gate.shape
    y_hi, z, x = (lax.axis_index(name) for name in ("y_hi", "z", "x"))
    place = jnp.stack([lax.axis_index("y_lo"), lax.axis_index("core")])
    block = (y_hi * Z + z) * X + x
    parts = width // CHUNK
    bf16 = jnp.bfloat16
    places = []
    blocks = 1
    for _, _, partners in STAGES:
        ways = len(partners) + 1
        mine = block // blocks % ways
        for other in (0,) + tuple(other for _, other in partners):
            member = mine ^ other
            after = (ways - 1 - member) * (blocks * ROWS)
            before = (mine - 1 - member) * (blocks * ROWS) + block % blocks * ROWS
            places += [-after.astype(jnp.float32), -jnp.maximum(before, 0).astype(jnp.float32), (member < mine).astype(jnp.float32)]
        blocks *= ways
    pre_gate, place, *places = lax.optimization_barrier((pre_gate, place, *places))
    total, inner, rates, weights, skips = pl.pallas_call(
        states_kernel,
        in_specs=[ANY] * 5,
        out_specs=[VMEM] * 5,
        out_shape=[
            shape_of((MODES, width)),
            shape_of((rows, width), bf16),
            shape_of((MODES, width)),
            shape_of((MODES, width)),
            shape_of((1, width)),
        ],
        scratch_shapes=[
            pltpu.VMEM((rows, width), bf16),
            pltpu.VMEM((rows, width), bf16),
            pltpu.VMEM((MODES, width), jnp.float32),
            pltpu.SemaphoreType.DMA((parts, 5)),
        ],
        name="states",
        compiler_params=PARAMS,
    )(*(in_hbm(a) for a in (pre_gate, values, decay_rates.T, residues.T, skip_gain[None, :])))

    def local(part, inner):
        outs = [shape_of((rows, CHUNK))] + [shape_of((width, CHUNK), bf16)] * (2 * CORE) + [shape_of((rows, CHUNK), bf16)]
        return pl.pallas_call(
            functools.partial(fetching_kernel, first_tile=part * (CHUNK // LANES)),
            in_specs=[SMEM, ANY, ANY] + [VMEM] * 4,
            out_specs=[VMEM] * len(outs),
            out_shape=outs,
            scratch_shapes=[pltpu.VMEM((rows, LANES), jnp.float32)] * 3 + [pltpu.SemaphoreType.DMA((len(outs),))],
            cost_estimate=LOCAL_COST,
            name="local",
            compiler_params=PARAMS,
        )(place, in_hbm(out_weight), in_hbm(post_gate), *(in_vmem(a) for a in (inner, rates, weights, skips)))

    group = total
    carry = jnp.zeros_like(total)
    pieces = []
    for step, (axis, size, partners) in enumerate(STAGES):
        others = [
            lax.ppermute(group.astype(bf16), axis, [(i, i ^ flip) for i in range(size)]).astype(jnp.float32)
            for flip, _ in partners
        ]
        after, _, _ = places[:3]
        group = jnp.exp(after * rates) * group
        for n, other in enumerate(others):
            after, before, earlier = places[3 * n + 3 : 3 * n + 6]
            group = group + jnp.exp(after * rates) * other
            carry = carry + earlier * jnp.exp(before * rates) * other
        places = places[3 * len(others) + 3 :]
        part = step - (len(STAGES) - parts)
        if part >= 0:
            piece = local(part, inner)
            group, carry, *piece = lax.optimization_barrier((group, carry, *piece))
            pieces.append(piece)
        inner, group, carry = lax.optimization_barrier((inner, group, carry))
    locals_, *roles, posts = (list(part) for part in zip(*pieces))
    arrays = (carry, rates, weights, *locals_, *posts, *roles[0])
    gated, sent = pl.pallas_call(
        mix_kernel,
        in_specs=[VMEM] * len(arrays),
        out_specs=[VMEM] * 2,
        out_shape=[shape_of((rows, width), bf16), shape_of((rows, width), bf16)],
        scratch_shapes=[pltpu.VMEM((rows, width), jnp.float32)],
        cost_estimate=COST,
        name="mix",
        compiler_params=PARAMS,
    )(*(in_vmem(a) for a in arrays))
    kept = pl.pallas_call(
        own_kernel,
        in_specs=[VMEM] * (1 + parts),
        out_specs=VMEM,
        out_shape=shape_of((rows, width)),
        cost_estimate=COST,
        name="own",
        compiler_params=PARAMS,
    )(*(in_vmem(a) for a in (gated, *roles[1])))

    def swap(array, axis):
        return lax.ppermute(array.astype(jnp.bfloat16), axis, [(0, 1), (1, 0)]).astype(jnp.float32)

    to_far = (swap(sent, "core") + kept).astype(bf16)
    gated, to_far = lax.optimization_barrier((gated, to_far))
    far_sum = swap(to_far, "y_lo")
    sent, kept = pl.pallas_call(
        near_kernel,
        in_specs=[VMEM] * (1 + 2 * parts),
        out_specs=[VMEM] * 2,
        out_shape=[shape_of((rows, width), bf16), shape_of((rows, width))],
        cost_estimate=COST,
        name="near",
        compiler_params=PARAMS,
    )(*(in_vmem(a) for a in (gated, *roles[2], *roles[3])))
    quarter = rows // 4
    received = [swap(sent[i : i + quarter], "core") for i in range(0, rows, quarter)]
    near_sum = lax.optimization_barrier(jnp.concatenate(received, axis=0) + kept)
    return (near_sum + far_sum).astype(bf16)


def solution(mesh):
    axes = ("y_hi", "z", "x", "y_lo", "core")
    split = Mesh(mesh.devices.reshape(Y_HI, Z, X, Y_LO, CORE), axes)
    seq, chan = axes[:3], axes[3:]
    placed = (P(seq, chan), P(seq, chan), P(seq, chan), P(chan, None), P(chan, None), P(chan), P(chan, None))
    return jax.shard_map(body, mesh=split, in_specs=placed, out_specs=P(seq, chan), check_vma=False)
```

```python
import functools

import jax
import jax.numpy as jnp
from jax import lax
from jax.experimental import pallas as pl
from jax.experimental.pallas import tpu as pltpu
from jax.sharding import Mesh
from jax.sharding import PartitionSpec as P

Y_HI, Z, X, Y_LO, CORE = 2, 8, 4, 2, 2
MODES = 16
ROWS = 256
SUBS = 8
STEPS = ROWS // SUBS
LANES = 128
CHUNK = 256
ANY = pl.BlockSpec(memory_space=pl.ANY)
VMEM = pl.BlockSpec(memory_space=pltpu.VMEM)
SMEM = pl.BlockSpec(memory_space=pltpu.SMEM)
STAGES = (
    ("x", X, ((1, 1), (3, 3), (2, 2))),
    ("z", Z, ((1, 1), (3, 3), (2, 2))),
    ("z", Z, ((6, 1),)),
    ("y_hi", Y_HI, ((1, 1),)),
)
LOCAL_COST = pl.CostEstimate(flops=10**8, bytes_accessed=2**20, transcendentals=0)
COST = pl.CostEstimate(flops=2 * 10**9, bytes_accessed=4 * 2**20, transcendentals=0)
PARAMS = pltpu.CompilerParams(vmem_limit_bytes=16 * 2**20)


def in_hbm(array):
    return pltpu.with_memory_space_constraint(array, pltpu.HBM)


def in_vmem(array):
    return pltpu.with_memory_space_constraint(array, pltpu.VMEM)


def shape_of(shape, dtype=jnp.float32):
    return jax.ShapeDtypeStruct(shape, dtype)


def rows8(row):
    return jnp.broadcast_to(row, (SUBS, row.shape[-1]))


def add_all(terms):
    terms = list(terms)
    while len(terms) > 1:
        terms = [a + b for a, b in zip(terms[::2], terms[1::2])] + terms[len(terms) & ~1 :]
    return terms[0]


def tile_of(index):
    if isinstance(index, int):
        return pl.ds(index * LANES, LANES)
    return pl.ds(pl.multiple_of(index * LANES, LANES), LANES)


def expm1(value):
    series = jnp.ones_like(value)
    for n in range(9, 1, -1):
        series = 1.0 + value * (1.0 / n) * series
    return jnp.where(jnp.abs(value) < 0.25, value * series, jnp.exp(value) - 1.0)


def states_kernel(
    pre_hbm, val_hbm, rate_hbm, residue_hbm, skip_hbm,
    total_ref, inner_ref, rate_ref, weight_ref, skip_ref, pre_buf, val_buf, residue_buf, sems
):
    width = pre_hbm.shape[1]
    pairs = ((rate_hbm, rate_ref), (pre_hbm, pre_buf), (val_hbm, val_buf), (residue_hbm, residue_buf), (skip_hbm, skip_ref))
    copies = []
    for start in range(0, width, CHUNK):
        part = pl.ds(start, CHUNK)
        n = len(copies)
        copies.append(
            [pltpu.make_async_copy(hbm.at[:, part], buf.at[:, part], sems.at[n, j]) for j, (hbm, buf) in enumerate(pairs)]
        )
        for copy in copies[-1]:
            copy.start()
    left = (SUBS - 1 - lax.broadcasted_iota(jnp.int32, (SUBS, LANES), 0)).astype(jnp.float32)

    def tile(index):
        cols = tile_of(index)
        decay = jnp.exp(-float(SUBS) * rate_ref[:, cols])
        factors = [rows8(decay[m : m + 1]) for m in range(MODES)]
        states = None
        for start in range(0, ROWS, 2 * SUBS):
            rows = pl.ds(start, 2 * SUBS)
            product = pre_buf[rows, cols].astype(jnp.float32) * val_buf[rows, cols].astype(jnp.float32)
            product = product.astype(jnp.bfloat16)
            inner_ref[rows, cols] = product
            value = product.astype(jnp.float32)
            for half in (value[:SUBS], value[SUBS:]):
                if states is None:
                    states = [half] * MODES
                else:
                    states = [f * s + half for f, s in zip(factors, states)]
        totals = []
        for m in range(MODES):
            weight = jnp.exp(-rows8(rate_ref[m : m + 1, cols]) * left)
            totals.append(jnp.sum(states[m] * weight, axis=0, keepdims=True))
        total_ref[:, cols] = jnp.concatenate(totals, axis=0)
        weight_ref[:, cols] = residue_buf[:, cols] * jnp.sqrt(-expm1(-2.0 * rate_ref[:, cols]))

    for n, group in enumerate(copies):
        for copy in group:
            copy.wait()
        pl.loop(n * (CHUNK // LANES), (n + 1) * (CHUNK // LANES))(tile)


def local_kernel(inner_ref, rate_ref, weight_ref, skip_ref, out_ref, inner_buf, taps_buf, sums_buf, *, first_tile):
    lag = lax.broadcasted_iota(jnp.int32, (STEPS, LANES), 0).astype(jnp.float32)
    start = lax.broadcasted_iota(jnp.int32, (STEPS, LANES), 0) == 0
    where = lax.broadcasted_iota(jnp.int32, (SUBS, LANES), 0)

    def at(step):
        return inner_buf[pl.ds(step, SUBS, stride=STEPS), :]

    def tile(index):
        here = tile_of(index)
        cols = tile_of(index + first_tile)
        inner_buf[...] = inner_ref[:, cols].astype(jnp.float32)
        taps = jnp.where(start, skip_ref[:, cols], 0.0)
        for m in range(MODES):
            taps = taps + weight_ref[m : m + 1, cols] * jnp.exp(-rate_ref[m : m + 1, cols] * lag)
        for step in range(STEPS):
            taps_buf[pl.ds(step * SUBS, SUBS), :] = rows8(taps[step : step + 1])
        decay = jnp.exp(-rate_ref[:, cols])
        factors = [rows8(decay[m : m + 1]) for m in range(MODES)]
        states = [at(0)] * MODES
        for step in range(1, STEPS):
            value = at(step)
            states = [f * s + value for f, s in zip(factors, states)]
        entering = []
        for m in range(MODES):
            rate = rows8(rate_ref[m : m + 1, cols])
            state = states[m]
            span = 1
            while span < SUBS:
                moved = jnp.where(where >= span, pltpu.roll(state, span, 0), 0.0)
                state = state + jnp.exp(-rate * float(span * STEPS)) * moved
                span *= 2
            state = jnp.where(where >= 1, pltpu.roll(state, 1, 0), 0.0)
            entering.append(state * factors[m] * rows8(weight_ref[m : m + 1, cols]))
        for base in range(0, STEPS, SUBS):
            sums = []
            for _ in range(SUBS):
                sums.append(add_all(entering))
                entering = [f * e for f, e in zip(factors, entering)]
            for source in range(base + SUBS):
                value = at(source)
                for j in range(max(0, source - base), SUBS):
                    tap = taps_buf[pl.ds((base + j - source) * SUBS, SUBS), :]
                    sums[j] = sums[j] + tap * value
            for j in range(SUBS):
                sums_buf[pl.ds(base + j, SUBS, stride=STEPS), :] = sums[j]
        out_ref[:, here] = sums_buf[...]

    pl.loop(0, out_ref.shape[1] // LANES)(tile)


def first_column(place_ref, role, width):
    y_lo, core = place_ref[0], place_ref[1]
    chip = y_lo if role >= CORE else 1 - y_lo
    to_core = core if role % CORE else 1 - core
    return pl.multiple_of((chip * CORE + to_core) * width, width)


def fetching_kernel(place_ref, proj_hbm, post_hbm, inner_ref, rate_ref, weight_ref, skip_ref, out_ref, *refs, first_tile):
    *roles, post_ref, inner_buf, taps_buf, sums_buf, sems = refs
    width, part = roles[0].shape
    cols = pl.ds(first_tile * LANES, part)
    copies = [pltpu.make_async_copy(post_hbm.at[:, cols], post_ref, sems.at[len(roles)])]
    for role, role_ref in enumerate(roles):
        start = pl.multiple_of(first_column(place_ref, role, width) + first_tile * LANES, part)
        copies.append(pltpu.make_async_copy(proj_hbm.at[:, pl.ds(start, part)], role_ref, sems.at[role]))
    for copy in copies:
        copy.start()
    buffers = (inner_buf, taps_buf, sums_buf)
    local_kernel(inner_ref, rate_ref, weight_ref, skip_ref, out_ref, *buffers, first_tile=first_tile)
    for copy in copies:
        copy.wait()


def project(gated_ref, proj_refs, out_ref):
    start = 0
    for proj_ref in proj_refs:
        part = proj_ref.shape[1]
        sums = jnp.dot(gated_ref[...], proj_ref[...], preferred_element_type=jnp.float32)
        out_ref[:, start : start + part] = sums.astype(out_ref.dtype)
        start += part


def mix_kernel(carry_ref, rate_ref, weight_ref, *refs):
    *refs, gated_ref, sent_ref, sums_buf = refs
    parts = len(refs) // 3
    local_refs, post_refs, proj_refs = refs[:parts], refs[parts : 2 * parts], refs[2 * parts :]
    rows_count = gated_ref.shape[0]
    ahead = (lax.broadcasted_iota(jnp.int32, (SUBS, LANES), 0) + 1).astype(jnp.float32)

    def tile(index, local_ref, post_ref, offset):
        here = tile_of(index)
        cols = tile_of(index + offset)
        carry = carry_ref[:, cols] * weight_ref[:, cols]
        decay = jnp.exp(-float(SUBS) * rate_ref[:, cols])
        terms = []
        factors = []
        for m in range(MODES):
            rate = rows8(rate_ref[m : m + 1, cols])
            terms.append(jnp.exp(-rate * ahead) * rows8(carry[m : m + 1]))
            factors.append(rows8(decay[m : m + 1]))
        for start in range(0, rows_count, 2 * SUBS):
            sums = []
            for _ in range(2):
                sums.append(add_all(terms))
                terms = [f * t for f, t in zip(factors, terms)]
            rows = pl.ds(start, 2 * SUBS)
            conv = local_ref[rows, here] + jnp.concatenate(sums, axis=0)
            gated_ref[rows, cols] = (post_ref[rows, here].astype(jnp.float32) * conv).astype(jnp.bfloat16)

    each = local_refs[0].shape[1] // LANES
    deep = each * LANES

    def add_product(part):
        cols = slice(part * deep, (part + 1) * deep)
        gated = gated_ref[:, cols]
        for n, proj_ref in enumerate(proj_refs):
            into = slice(n * proj_ref.shape[1], (n + 1) * proj_ref.shape[1])
            sums = jnp.dot(gated, proj_ref[cols, :], preferred_element_type=jnp.float32)
            if part:
                sums = sums + sums_buf[:, into]
            if part < parts - 1:
                sums_buf[:, into] = sums
            else:
                sent_ref[:, into] = sums.astype(sent_ref.dtype)

    for part in range(parts):
        if part:
            add_product(part - 1)
        for i in range(each):
            tile(i, local_refs[part], post_refs[part], part * each)
    add_product(parts - 1)


def own_kernel(gated_ref, *refs):
    *proj_refs, kept_ref = refs
    project(gated_ref, proj_refs, kept_ref)


def near_kernel(gated_ref, *refs):
    *proj_refs, sent_ref, kept_ref = refs
    parts = len(proj_refs) // 2
    project(gated_ref, proj_refs[:parts], sent_ref)
    project(gated_ref, proj_refs[parts:], kept_ref)


def body(pre_gate, post_gate, values, decay_rates, residues, skip_gain, out_weight):
    rows, width = pre_gate.shape
    y_hi, z, x = (lax.axis_index(name) for name in ("y_hi", "z", "x"))
    place = jnp.stack([lax.axis_index("y_lo"), lax.axis_index("core")])
    block = (y_hi * Z + z) * X + x
    parts = width // CHUNK
    bf16 = jnp.bfloat16
    places = []
    blocks = 1
    for _, _, partners in STAGES:
        ways = len(partners) + 1
        mine = block // blocks % ways
        for other in (0,) + tuple(other for _, other in partners):
            member = mine ^ other
            after = (ways - 1 - member) * (blocks * ROWS)
            before = (mine - 1 - member) * (blocks * ROWS) + block % blocks * ROWS
            places += [-after.astype(jnp.float32), -jnp.maximum(before, 0).astype(jnp.float32), (member < mine).astype(jnp.float32)]
        blocks *= ways
    pre_gate, place, *places = lax.optimization_barrier((pre_gate, place, *places))
    total, inner, rates, weights, skips = pl.pallas_call(
        states_kernel,
        in_specs=[ANY] * 5,
        out_specs=[VMEM] * 5,
        out_shape=[
            shape_of((MODES, width)),
            shape_of((rows, width), bf16),
            shape_of((MODES, width)),
            shape_of((MODES, width)),
            shape_of((1, width)),
        ],
        scratch_shapes=[
            pltpu.VMEM((rows, width), bf16),
            pltpu.VMEM((rows, width), bf16),
            pltpu.VMEM((MODES, width), jnp.float32),
            pltpu.SemaphoreType.DMA((parts, 5)),
        ],
        name="states",
        compiler_params=PARAMS,
    )(*(in_hbm(a) for a in (pre_gate, values, decay_rates.T, residues.T, skip_gain[None, :])))

    def local(part, inner):
        outs = [shape_of((rows, CHUNK))] + [shape_of((width, CHUNK), bf16)] * (2 * CORE) + [shape_of((rows, CHUNK), bf16)]
        return pl.pallas_call(
            functools.partial(fetching_kernel, first_tile=part * (CHUNK // LANES)),
            in_specs=[SMEM, ANY, ANY] + [VMEM] * 4,
            out_specs=[VMEM] * len(outs),
            out_shape=outs,
            scratch_shapes=[pltpu.VMEM((rows, LANES), jnp.float32)] * 3 + [pltpu.SemaphoreType.DMA((len(outs),))],
            cost_estimate=LOCAL_COST,
            name="local",
            compiler_params=PARAMS,
        )(place, in_hbm(out_weight), in_hbm(post_gate), *(in_vmem(a) for a in (inner, rates, weights, skips)))

    group = total
    carry = jnp.zeros_like(total)
    pieces = []
    for step, (axis, size, partners) in enumerate(STAGES):
        others = [
            lax.ppermute(group.astype(bf16), axis, [(i, i ^ flip) for i in range(size)]).astype(jnp.float32)
            for flip, _ in partners
        ]
        after, _, _ = places[:3]
        group = jnp.exp(after * rates) * group
        for n, other in enumerate(others):
            after, before, earlier = places[3 * n + 3 : 3 * n + 6]
            group = group + jnp.exp(after * rates) * other
            carry = carry + earlier * jnp.exp(before * rates) * other
        places = places[3 * len(others) + 3 :]
        part = step - (len(STAGES) - parts)
        if part >= 0:
            piece = local(part, inner)
            group, carry, *piece = lax.optimization_barrier((group, carry, *piece))
            pieces.append(piece)
        inner, group, carry = lax.optimization_barrier((inner, group, carry))
    locals_, *roles, posts = (list(part) for part in zip(*pieces))
    arrays = (carry, rates, weights, *locals_, *posts, *roles[0])
    gated, sent = pl.pallas_call(
        mix_kernel,
        in_specs=[VMEM] * len(arrays),
        out_specs=[VMEM] * 2,
        out_shape=[shape_of((rows, width), bf16), shape_of((rows, width), bf16)],
        scratch_shapes=[pltpu.VMEM((rows, width), jnp.float32)],
        cost_estimate=COST,
        name="mix",
        compiler_params=PARAMS,
    )(*(in_vmem(a) for a in arrays))
    kept = pl.pallas_call(
        own_kernel,
        in_specs=[VMEM] * (1 + parts),
        out_specs=VMEM,
        out_shape=shape_of((rows, width)),
        cost_estimate=COST,
        name="own",
        compiler_params=PARAMS,
    )(*(in_vmem(a) for a in (gated, *roles[1])))

    def swap(array, axis):
        return lax.ppermute(array.astype(jnp.bfloat16), axis, [(0, 1), (1, 0)]).astype(jnp.float32)

    to_far = (swap(sent, "core") + kept).astype(bf16)
    gated, to_far = lax.optimization_barrier((gated, to_far))
    far_sum = swap(to_far, "y_lo")
    sent, kept = pl.pallas_call(
        near_kernel,
        in_specs=[VMEM] * (1 + 2 * parts),
        out_specs=[VMEM] * 2,
        out_shape=[shape_of((rows, width), bf16), shape_of((rows, width))],
        cost_estimate=COST,
        name="near",
        compiler_params=PARAMS,
    )(*(in_vmem(a) for a in (gated, *roles[2], *roles[3])))
    quarter = rows // 4
    received = [swap(sent[i : i + quarter], "core") for i in range(0, rows, quarter)]
    near_sum = lax.optimization_barrier(jnp.concatenate(received, axis=0) + kept)
    return (near_sum + far_sum).astype(bf16)


def solution(mesh):
    axes = ("y_hi", "z", "x", "y_lo", "core")
    split = Mesh(mesh.devices.reshape(Y_HI, Z, X, Y_LO, CORE), axes)
    seq, chan = axes[:3], axes[3:]
    placed = (P(seq, chan), P(seq, chan), P(seq, chan), P(chan, None), P(chan, None), P(chan), P(chan, None))
    return jax.shard_map(body, mesh=split, in_specs=placed, out_specs=P(seq, chan), check_vma=False)
```
